256 devices in a mesh: dp: 32 (over z, x), mp: 8 (over y, core).
Axes of the slice: x: 4, y: 4, z: 8, core: 2. Of those that a mesh axis runs over, the one named last changes fastest.
Arguments:
- tokens: bfloat16 [12288, 8192], P('dp', 'mp'), may hold values from -6 to 6
- frozen_base_weight: bfloat16 [8192, 8192], P('mp', 'dp'), may hold values from -0.0625 to 0.0625
- tenant_down_factors: bfloat16 [64, 8192, 64], P('dp', 'mp'), may hold values from -0.0625 to 0.0625
- tenant_up_factors: bfloat16 [64, 8192, 64], P('dp', 'mp'), may hold values from -0.75 to 0.75
- cotangent: bfloat16 [12288, 8192], P('dp', 'mp'), may hold values from -6 to 6
- block_tenant_index: int32 [96], replicated, may hold values from 0 to 63
- ranks: int32 [64], replicated, may hold values from 8 to 64
Outputs:
- layer_out: bfloat16 [12288, 8192], P('dp', 'mp')
- input_grad: bfloat16 [12288, 8192], P('dp', 'mp')
- down_grad: float32 [64, 8192, 64], P('dp', 'mp')
- up_grad: float32 [64, 8192, 64], P('dp', 'mp')
The draws below stay inside these ranges and needn't reach their ends.
Inputs may be any that keep to these rules, and one draw needn't show every extreme that they name: `block_tenant_index`: tenant of each block of 128 consecutive rows; some tenants own many blocks, some none. `ranks`: rank columns at or past a tenant's rank are unused.
All inputs are finite; a program needn't handle non-finite values.
Results may differ from the reference program's by a relative error of at most 0.017.
Values may be sent and summed in bfloat16 or wider, within the bound.
A program may use at most 128 MiB of HBM per device.

```python
import math
import jax
import jax.numpy as jnp
import numpy as np
from jax import lax

MODEL_WIDTH = 8192
PADDED_RANK = 64
BLOCK = 128
TENANT_TOTAL = 64
TOKENS = 12288
NBLK = 96
N_MP = 8


def with_ends(result, stream_key, least, largest):
    extent = result.shape
    index_at = [jax.random.randint(jax.random.fold_in(stream_key, axis), (), 0, extent[axis]) for axis in range(len(extent))]
    result = result.at[tuple(index_at)].set(least)
    longest = extent.index(max(extent))
    index_at[longest] = (index_at[longest] + 1) % extent[longest]
    return result.at[tuple(index_at)].set(largest)


def level_of(rng, extent, cuts, low, top_value):
    def one(axis_at, blocks):
        draws = jax.random.uniform(jax.random.fold_in(jax.random.fold_in(rng, 6), axis_at), (blocks,), jnp.float32, low / len(cuts), top_value / len(cuts))
        return jnp.repeat(jnp.exp(draws), extent[axis_at] // blocks).reshape((-1,) + (1,) * (len(extent) - axis_at - 1))

    factor_of = one(*cuts[0])
    for cut in cuts[1:]:
        factor_of = factor_of * one(*cut)
    return factor_of


def cumulative_ranks(count, slope):
    portions = [(1 << 20) // math.isqrt(rank ** slope) + 1 for rank in range(1, count + 1)]
    spread = 1 + sum(portions) // (1 << 30)
    return np.cumsum(np.array([max(1, weight // spread) for weight in portions]))


def ranked_ids(key, dims, amount, skew):
    listing = cumulative_ranks(amount, skew)
    pick = jax.random.randint(jax.random.fold_in(key, 1), dims, 0, int(listing[amount - 1]))
    standing = jnp.searchsorted(jnp.asarray(listing, jnp.int32), pick, side="right")
    return jax.random.permutation(jax.random.fold_in(key, 2), amount)[standing].astype(jnp.int32)


def normal_values(own_key, extent, spread, bound, cuts=(), held_as=jnp.bfloat16):
    entries = spread * jax.random.normal(own_key, extent, jnp.float32)
    if cuts:
        entries = entries * level_of(own_key, extent, cuts, -0.22, 0.18)
    return jnp.clip(entries, -bound, bound).astype(held_as)


def setup_inputs(seed: int = 0) -> dict:
    splits = jax.random.split(jax.random.key(seed), 8)
    tokens = normal_values(splits[0], (TOKENS, MODEL_WIDTH), 1.0, 6.0, ((0, 32), (1, 8)))
    frozen_base_weight = normal_values(splits[1], (MODEL_WIDTH, MODEL_WIDTH), MODEL_WIDTH ** -0.5, 0.0625, ((0, 8), (1, 32)))
    tenant_down_factors = normal_values(splits[2], (TENANT_TOTAL, MODEL_WIDTH, PADDED_RANK), MODEL_WIDTH ** -0.5, 0.0625, ((0, 32), (1, 8)))
    tenant_up_factors = normal_values(splits[3], (TENANT_TOTAL, MODEL_WIDTH, PADDED_RANK), PADDED_RANK ** -0.5, 0.75, ((0, 32), (1, 8)))
    cotangent = normal_values(splits[4], (TOKENS, MODEL_WIDTH), 1.0, 6.0, ((0, 32), (1, 8)))
    block_tenant_index = with_ends(ranked_ids(splits[5], (NBLK,), TENANT_TOTAL, 2), jax.random.fold_in(splits[5], 3), 0, TENANT_TOTAL - 1).astype(jnp.int32)
    ranks = with_ends(jax.random.randint(splits[6], (TENANT_TOTAL,), 8, PADDED_RANK + 1), jax.random.fold_in(splits[6], 1), 8, PADDED_RANK).astype(jnp.int32)
    return {"tokens": tokens, "frozen_base_weight": frozen_base_weight, "tenant_down_factors": tenant_down_factors, "tenant_up_factors": tenant_up_factors, "cotangent": cotangent, "block_tenant_index": block_tenant_index, "ranks": ranks}


def reference(tokens, frozen_base_weight, tenant_down_factors, tenant_up_factors, cotangent, block_tenant_index, ranks):
    count_of_tenants = tenant_down_factors.shape[0]
    block_total = block_tenant_index.shape[0]
    row_total = tokens.shape[0]
    positions = jnp.arange(PADDED_RANK, dtype=jnp.int32)
    kept = (positions[None, :] < ranks[:, None]).astype(jnp.float32)
    coef = kept * (16.0 / ranks.astype(jnp.float32))[:, None]
    block_coef = coef[block_tenant_index]
    tok_blocks = tokens.reshape(block_total, BLOCK, MODEL_WIDTH).astype(jnp.float32)
    cot_blocks = cotangent.reshape(block_total, BLOCK, MODEL_WIDTH).astype(jnp.float32)
    chosen_down_factor = tenant_down_factors[block_tenant_index].astype(jnp.float32)
    chosen_up_factor = tenant_up_factors[block_tenant_index].astype(jnp.float32)
    pre_low = jnp.einsum("bid,bdr->bir", tok_blocks, chosen_down_factor)
    low = (pre_low * block_coef[:, None, :]).astype(jnp.bfloat16)
    span = MODEL_WIDTH // N_MP
    base = jnp.zeros((row_total, MODEL_WIDTH), jnp.float32)
    for portion in range(N_MP):
        term = jnp.dot(tokens[:, portion * span:(portion + 1) * span],
                       frozen_base_weight[portion * span:(portion + 1) * span, :],
                       preferred_element_type=jnp.float32)
        rounded = lax.optimization_barrier(term.astype(jnp.bfloat16))
        base = base + rounded.astype(jnp.float32)
    adapter = jnp.einsum("bir,ber->bie", low.astype(jnp.float32), chosen_up_factor).reshape(row_total, MODEL_WIDTH)
    layer_out = (base + adapter).astype(jnp.bfloat16)
    pre_dlow = jnp.einsum("bie,ber->bir", cot_blocks, chosen_up_factor)
    dlow = (pre_dlow * block_coef[:, None, :]).astype(jnp.bfloat16)
    base_grad = jnp.dot(cotangent, frozen_base_weight.T, preferred_element_type=jnp.float32)
    adapter_grad = jnp.einsum("bir,bdr->bid", dlow.astype(jnp.float32), chosen_down_factor).reshape(row_total, MODEL_WIDTH)
    input_grad = (base_grad + adapter_grad).astype(jnp.bfloat16)
    block_down = jnp.einsum("bid,bir->bdr", tok_blocks, dlow.astype(jnp.float32))
    block_up = jnp.einsum("bie,bir->ber", cot_blocks, low.astype(jnp.float32))
    onehot = (block_tenant_index[None, :] == jnp.arange(count_of_tenants, dtype=jnp.int32)[:, None]).astype(jnp.float32)
    down_grad = jnp.einsum("tb,bdr->tdr", onehot, block_down, precision=lax.Precision.HIGHEST)
    up_grad = jnp.einsum("tb,ber->ter", onehot, block_up, precision=lax.Precision.HIGHEST)
    return layer_out, input_grad, down_grad, up_grad
```

```python
import functools

import jax
import jax.numpy as jnp
from jax import lax
from jax.experimental import pallas as pl
from jax.experimental.pallas import tpu as pltpu
from jax.sharding import PartitionSpec as P

MESH = pl.DeviceIdType.MESH
BF = jnp.bfloat16
F32 = jnp.float32
NZ, NX, NY = 8, 4, 4
NT = (((1,), (1,)), ((), ()))


def kernel(
    idx, ranks, tok, w, dn, up, cot,
    o_y, o_g, o_dg, o_ug,
    fs, ft, ss, fac, gs, gr, sel, hs, hr, lp, lr, lo,
    wg, xg, cg, yp, yr, ys, yf, gp, gg, ge, gx,
    s_l, r_l, s_wa, r_wa, s_wb, r_wb, s_wc, r_wc, s_x, r_x, s_c, r_c, s_ca, r_ca,
    s_y, r_y, s_ya, r_ya, s_g, r_g, s_gx, r_gx, s_m, r_m, s_loc,
):
    dp = lax.axis_index("dp")
    mp = lax.axis_index("mp")
    z, x = dp // NX, dp % NX
    y, c = mp // 2, mp % 2
    o = 1 - c
    turn = 1 - 2 * c

    def dev(zz, xx, yy, cc):
        return (zz * NX + xx, yy * 2 + cc)

    def start(src, dst, s_sem, r_sem, device):
        copy = pltpu.make_async_remote_copy(
            src_ref=src, dst_ref=dst, send_sem=s_sem, recv_sem=r_sem,
            device_id=device, device_id_type=MESH,
        )
        copy.start()

    def wait(ref, sem):
        pltpu.make_async_copy(ref, ref, sem).wait()

    def ranks_at(i):
        return pl.ds(pl.multiple_of(16 * i, 16), 16)

    def lanes_at(i):
        return pl.ds(pl.multiple_of(256 * i, 256), 256)

    def half(i):
        return pl.ds(pl.multiple_of(192 * i, 192), 192)

    def dp_peer(k):
        return (z + k // NX) % NZ, (x + k % NX) % NX

    barrier = pltpu.get_barrier_semaphore()

    def greet_dp(k, carry):
        pz, px = dp_peer(k)
        pl.semaphore_signal(barrier, inc=1, device_id=dev(pz, px, y, c), device_id_type=MESH)
        return carry

    def greet_mp(k, carry):
        pl.semaphore_signal(barrier, inc=1, device_id=(dp, (mp + k) % 8), device_id_type=MESH)
        return carry

    def greet_x(k, carry):
        pl.semaphore_signal(barrier, inc=1, device_id=dev(z, (x + k) % NX, y, o), device_id_type=MESH)
        return carry

    lax.fori_loop(1, 32, greet_dp, 0)
    lax.fori_loop(1, 8, greet_mp, 0)
    lax.fori_loop(1, 4, greet_x, 0)

    for j in range(8):
        src = dn if j < 4 else up
        r0 = 16 * (j % 4)
        for i in range(4):
            fs[4 * j + i] = src[:, r0:r0 + 16, 256 * i:256 * i + 256]

    pl.semaphore_wait(barrier, 41)

    def spread(k, carry):
        pz, px = dp_peer(k)
        start(fs.at[pz * NX + px], ft.at[pl.ds(2 * dp, 2)], s_l.at[0], r_l.at[0], dev(pz, px, y, c))
        return carry

    lax.fori_loop(1, 32, spread, 0)
    za, zb = (z + turn + NZ) % NZ, (z - turn + NZ) % NZ
    start(w, wg.at[z, c], s_wa.at[0], r_wa.at[0], dev(za, x, y, c))
    start(w, wg.at[z, c], s_wb.at[0], r_wb.at[0], dev(zb, x, y, c))
    start(w, wg.at[z, c], s_wc.at[0], r_wc.at[0], dev(z, x, y, o))
    xr, xl = (x + 1) % NX, (x + 3) % NX
    for h in range(2):
        rows = tok.at[pl.ds(192 * h, 192)]
        start(rows, xg.at[c, x], s_x.at[h], r_x.at[c], dev(z, xr, y, h))
        start(rows, xg.at[c, x], s_x.at[2 + h], r_x.at[2 + c], dev(z, xl, y, h))
    start(tok.at[half(o)], xg.at[c, x], s_x.at[4], r_x.at[4], dev(z, x, y, o))

    def cot_out(j, carry):
        px, ph = (x + j // 2) % NX, (c + j % 2) % 2
        start(cot.at[half(ph), lanes_at(px)], cg.at[mp, x], s_c.at[j], r_c.at[j], dev(z, px, y, ph))
        return carry

    lax.fori_loop(1, 8, cot_out, 0)
    loc = [
        pltpu.make_async_copy(w, wg.at[z, c], s_loc.at[0]),
        pltpu.make_async_copy(tok.at[half(c)], xg.at[c, x], s_loc.at[1]),
        pltpu.make_async_copy(cot.at[half(c), lanes_at(x)], cg.at[mp, x], s_loc.at[2]),
        pltpu.make_async_copy(fs.at[dp], ft.at[pl.ds(2 * dp, 2)], s_loc.at[3]),
    ]
    for copy in loc:
        copy.start()

    lane = lax.broadcasted_iota(jnp.int32, (8, 1536), 1)

    def place(b, carry):
        return jnp.where(lane // 16 == b, idx[b] * 16 + lane % 16, carry)

    owner_row = lax.fori_loop(0, 96, place, jnp.zeros((8, 1536), jnp.int32))[0:1]

    def fill(i, carry):
        at = lax.broadcasted_iota(jnp.int32, (64, 1536), 0) + i * 64
        sel[pl.ds(pl.multiple_of(i * 64, 64), 64), :] = jnp.where(at == owner_row, 1.0, 0.0).astype(BF)
        return carry

    lax.fori_loop(0, 16, fill, 0)
    for copy in loc:
        copy.wait()

    for j in range(1, 8):
        wait(cg.at[0, 0], r_c.at[j])
    own = cg.at[pl.ds(2 * y, 2)]
    for d in range(1, 4):
        start(own, own, s_ca.at[d - 1], r_ca.at[d - 1], dev(z, x, (y + d) % NY, c))

    wait(xg.at[0, 0], r_x.at[0])
    start(xg.at[0, xl], xg.at[0, xl], s_x.at[5], r_x.at[5], dev(z, xr, y, c))
    wait(xg.at[0, 0], r_x.at[3])
    start(xg.at[1, xr], xg.at[1, xr], s_x.at[6], r_x.at[6], dev(z, xl, y, c))

    def ring(k):
        ca, cb = (z - turn * k + NZ) % NZ, (z + turn * k + NZ) % NZ
        wait(w, r_wa.at[k - 1])
        if k < 4:
            start(wg.at[ca, c], wg.at[ca, c], s_wa.at[k], r_wa.at[k], dev(za, x, y, c))
        start(wg.at[ca, c], wg.at[ca, c], s_wc.at[k], r_wc.at[k], dev(z, x, y, o))
        if k < 4:
            wait(w, r_wb.at[k - 1])
            if k < 3:
                start(wg.at[cb, c], wg.at[cb, c], s_wb.at[k], r_wb.at[k], dev(zb, x, y, c))
            start(wg.at[cb, c], wg.at[cb, c], s_wc.at[4 + k], r_wc.at[4 + k], dev(z, x, y, o))

    def forward(zc):
        acc = jnp.dot(xg[0].reshape(768, 1024), wg[zc, 0], preferred_element_type=F32)
        acc = acc + jnp.dot(xg[1].reshape(768, 1024), wg[zc, 1], preferred_element_type=F32)
        yp[zc] = acc.astype(BF)
        yd = zc // 2

        @pl.when(yd != y)
        def _():
            slot = ((y - yd + NY) % NY - 1) * 2 + zc % 2
            start(yp.at[zc], yr.at[slot], s_y.at[0], r_y.at[0], dev(z, x, yd, c))

    def forward_pair(k):
        wait(w, r_wc.at[4 + k])
        wait(w, r_wc.at[k])

        def one(i, carry):
            forward((z + (2 * i - 1) * turn * k + NZ) % NZ)
            return carry

        lax.fori_loop(0, 2, one, 0)

    ring(1)

    wait(ft.at[pl.ds(0, 62)], r_l.at[0])

    def select(k, carry):
        pz, px = dp_peer(k)
        p = pz * NX + px
        for s in range(3):
            ss[3 * p + s] = ft[idx[3 * p + s]]
        return carry

    lax.fori_loop(0, 32, select, 0)

    def send_selected(k, carry):
        pz, px = dp_peer(k)
        start(ss.at[pl.ds(3 * (pz * NX + px), 3)], fac.at[:, ranks_at(z), lanes_at(x)],
              s_l.at[1], r_l.at[1], dev(pz, px, y, c))
        return carry

    lax.fori_loop(1, 32, send_selected, 0)
    own_sel = pltpu.make_async_copy(
        ss.at[pl.ds(3 * dp, 3)], fac.at[:, ranks_at(z), lanes_at(x)], s_loc.at[0])
    own_sel.start()

    ring(2)
    for j in (1, 2, 4, 5, 6):
        wait(xg.at[0, 0], r_x.at[j])
    wait(w, r_wc.at[0])
    forward(z)
    forward_pair(1)
    own_sel.wait()

    wait(ss.at[pl.ds(0, 93)], r_l.at[1])
    for s in range(3):
        rows = slice(128 * s, 128 * s + 128)
        a = lax.dot_general(tok[rows], fac[s, 0:64], NT, preferred_element_type=F32)
        b = lax.dot_general(cot[rows], fac[s, 64:128], NT, preferred_element_type=F32)
        lp[rows] = jnp.concatenate([a, b], axis=1)

    def piece(m):
        return pl.ds(pl.multiple_of(48 * m, 16), 48)

    def send_low(k, carry):
        m = (mp + k) % 8
        start(lp.at[piece(m)], lr.at[mp], s_m.at[0], r_m.at[0], (dp, m))
        return carry

    lax.fori_loop(1, 8, send_low, 0)
    lr[mp] = lp[piece(mp)]
    wait(lr.at[pl.ds(0, 7)], r_m.at[0])
    total = lr[0]
    for m in range(1, 8):
        total = total + lr[m]
    rank_lane = lax.broadcasted_iota(jnp.int32, (16, 128), 1) % 64
    coefs = []
    for g in range(3):
        block = dp * 3 + (mp * 48 + 16 * g) // 128
        held = jnp.full((16, 128), ranks[idx[block]], jnp.int32)
        coefs.append(jnp.where(rank_lane < held, 16.0 / held.astype(F32), 0.0))
    lo[piece(mp)] = (total * jnp.concatenate(coefs, axis=0)).astype(BF)

    def send_lo(k, carry):
        m = (mp + k) % 8
        start(lo.at[piece(mp)], lo.at[piece(mp)], s_m.at[1], r_m.at[1], (dp, m))
        return carry

    lax.fori_loop(1, 8, send_lo, 0)

    ring(3)
    wait(lo.at[pl.ds(0, 336)], r_m.at[1])

    for s in range(3):
        rows = slice(128 * s, 128 * s + 128)
        turned = lo[rows].astype(F32).T.astype(BF)
        gs[s, 0:64] = jnp.dot(turned[64:128], tok[rows], preferred_element_type=F32).astype(BF)
        gs[s, 64:128] = jnp.dot(turned[0:64], cot[rows], preferred_element_type=F32).astype(BF)

    def send_grads(k, carry):
        pz, px = dp_peer(k)
        start(gs.at[:, ranks_at(pz), lanes_at(px)], gr.at[pl.ds(3 * dp, 3)],
              s_l.at[2], r_l.at[2], dev(pz, px, y, c))
        return carry

    lax.fori_loop(1, 32, send_grads, 0)
    own_grads = pltpu.make_async_copy(
        gs.at[:, ranks_at(z), lanes_at(x)], gr.at[pl.ds(3 * dp, 3)], s_loc.at[1])
    own_grads.start()

    forward_pair(2)
    ring(4)
    forward_pair(3)
    wait(w, r_wc.at[4])
    forward((z + 4) % NZ)

    for d in range(3):
        wait(cg.at[pl.ds(0, 2)], r_ca.at[d])

    def backward(t, carry):
        acc = jnp.zeros((768, 256), F32)
        for n in range(8):
            acc = acc + lax.dot_general(
                cg[n].reshape(768, 256), wg[n, t // 4, lanes_at(t % 4), :], NT,
                preferred_element_type=F32)
        gp[t] = acc.astype(BF).reshape(4, 192, 256)
        for d in (2, 1, 3):
            px = (x + d) % NX
            start(gp.at[t, px], gg.at[3 - d, t], s_g.at[d - 1], r_g.at[3 - d, t], dev(z, px, y, c))
        return carry

    lax.fori_loop(0, 8, backward, 0)

    wait(yr, r_y.at[0])

    def sum_y(i, carry):
        cc, px = i // 4, i % 4
        rows = pl.ds(pl.multiple_of(192 * px, 192), 192)
        acc = yp[2 * y + cc, rows].astype(F32)
        for d in range(3):
            acc = acc + yr[2 * d + cc, rows].astype(F32)
        ys[cc, px] = acc.astype(BF)
        return carry

    lax.fori_loop(0, 8, sum_y, 0)

    def send_base(j, carry):
        px, pc = (x + j // 2) % NX, (c + j % 2) % 2
        start(ys.at[pc, px], yf.at[c, :, lanes_at(x)], s_ya.at[j], r_ya.at[j], dev(z, px, y, pc))
        return carry

    lax.fori_loop(1, 8, send_base, 0)
    own_base = pltpu.make_async_copy(ys.at[c, x], yf.at[c, :, lanes_at(x)], s_loc.at[2])
    own_base.start()

    own_grads.wait()
    wait(gr.at[pl.ds(0, 93)], r_l.at[2])

    def sum_tenants(i, carry):
        rows = pl.ds(pl.multiple_of(256 * i, 256), 256)
        acc = jnp.dot(sel[rows, :], gr[...].reshape(1536, 256), preferred_element_type=F32)
        hs[pl.ds(16 * i, 16)] = acc.astype(BF).reshape(16, 16, 256)
        return carry

    lax.fori_loop(0, 4, sum_tenants, 0)

    def send_sums(k, carry):
        pz, px = dp_peer(k)
        start(hs.at[pl.ds(2 * (pz * NX + px), 2)], hr.at[:, ranks_at(z), lanes_at(x)],
              s_l.at[3], r_l.at[3], dev(pz, px, y, c))
        return carry

    lax.fori_loop(1, 32, send_sums, 0)
    own_sums = pltpu.make_async_copy(
        hs.at[pl.ds(2 * dp, 2)], hr.at[:, ranks_at(z), lanes_at(x)], s_loc.at[3])
    own_sums.start()

    own_base.wait()
    for j in range(1, 8):
        wait(ys.at[0, 0], r_ya.at[j])
    for u in range(6):
        rows = slice(64 * u, 64 * u + 64)
        acc = jnp.dot(lo[rows, 0:64], fac[u // 2, 64:128], preferred_element_type=F32)
        part = slice(64 * (u % 3), 64 * (u % 3) + 64)
        o_y[rows] = (acc + yf[u // 3, part].astype(F32)).astype(BF)

    def sum_x(t):
        acc = gp[t, x].astype(F32)
        for d in range(3):
            acc = acc + gg[d, t].astype(F32)
        return acc

    for i in range(4):
        t = 4 * o + i
        for d in range(3):
            wait(gg.at[0, 0], r_g.at[d, t])
        ge[i] = sum_x(t).astype(BF)
        start(ge.at[i], gx.at[i], s_gx.at[i], r_gx.at[i], dev(z, x, y, o))
    for i in range(4):
        t = 4 * c + i
        for d in range(3):
            wait(gg.at[0, 0], r_g.at[d, t])

    def adapter_grad(h, i, q):
        rows = pl.ds(pl.multiple_of(192 * h + 64 * q, 64), 64)
        low = lo[rows, :][:, 64:128]
        return rows, jnp.dot(low, fac[(192 * h + 64 * q) // 128, 0:64, 256 * i:256 * i + 256],
                             preferred_element_type=F32)

    for i in range(4):
        total = sum_x(4 * c + i)
        for q in range(3):
            rows, acc = adapter_grad(c, i, q)
            o_g[rows, 256 * i:256 * i + 256] = (acc + total[64 * q:64 * q + 64]).astype(BF)
    for i in range(4):
        wait(ge.at[0], r_gx.at[i])
        for q in range(3):
            rows, acc = adapter_grad(o, i, q)
            part = gx[i, 64 * q:64 * q + 64].astype(F32)
            o_g[rows, 256 * i:256 * i + 256] = (acc + part).astype(BF)

    own_sums.wait()
    wait(hs.at[pl.ds(0, 62)], r_l.at[3])
    o_dg[...] = hr[:, 0:64].astype(F32)
    o_ug[...] = hr[:, 64:128].astype(F32)

    wait(ft.at[pl.ds(0, 62)], s_l.at[0])
    wait(ss.at[pl.ds(0, 93)], s_l.at[1])
    wait(gr.at[pl.ds(0, 93)], s_l.at[2])
    wait(hs.at[pl.ds(0, 62)], s_l.at[3])
    wait(lr.at[pl.ds(0, 7)], s_m.at[0])
    wait(lo.at[pl.ds(0, 336)], s_m.at[1])
    for k in range(4):
        wait(w, s_wa.at[k])
    for k in range(3):
        wait(w, s_wb.at[k])
    for k in range(8):
        wait(w, s_wc.at[k])
    for k in range(7):
        wait(xg.at[0, 0], s_x.at[k])
    for k in range(1, 8):
        wait(cg.at[0, 0], s_c.at[k])
        wait(ys.at[0, 0], s_ya.at[k])
    for d in range(3):
        wait(cg.at[pl.ds(0, 2)], s_ca.at[d])
        wait(gg.at[0], s_g.at[d])
    wait(yr, s_y.at[0])
    for i in range(4):
        wait(ge.at[0], s_gx.at[i])


def local(tokens, weight, down, up, cotangent, idx, ranks):
    down_t = jnp.swapaxes(down, 1, 2)
    up_t = jnp.swapaxes(up, 1, 2)
    vmem = pl.BlockSpec(memory_space=pltpu.VMEM)
    smem = pl.BlockSpec(memory_space=pltpu.SMEM)
    buf = lambda *shape: pltpu.VMEM(shape, BF)
    dma = lambda *shape: pltpu.SemaphoreType.DMA(shape)
    scratch = [
        buf(32, 2, 16, 256), buf(64, 16, 256), buf(96, 16, 256), buf(3, 128, 1024),
        buf(3, 128, 1024), buf(96, 16, 256), buf(1024, 1536), buf(64, 16, 256),
        buf(2, 128, 1024), pltpu.VMEM((384, 128), F32), pltpu.VMEM((8, 48, 128), F32),
        buf(384, 128),
        buf(8, 2, 1024, 256), buf(2, 4, 192, 1024), buf(8, 4, 192, 256),
        buf(8, 768, 256), buf(6, 768, 256), buf(2, 4, 192, 256), buf(2, 192, 1024),
        buf(8, 4, 192, 256), buf(3, 8, 192, 256), buf(4, 192, 256), buf(4, 192, 256),
        dma(4), dma(4), dma(4), dma(4), dma(3), dma(3), dma(8), dma(8), dma(7), dma(7),
        dma(8), dma(8), dma(3), dma(3),
        dma(1), dma(1), dma(8), dma(8), dma(3), dma(3, 8), dma(4), dma(4), dma(2), dma(2),
        dma(4),
    ]
    out = jax.ShapeDtypeStruct
    layer_out, input_grad, down_grad, up_grad = pl.pallas_call(
        kernel,
        out_shape=(
            out(tokens.shape, BF), out(cotangent.shape, BF),
            out(down_t.shape, F32), out(up_t.shape, F32),
        ),
        in_specs=[smem, smem] + [vmem] * 5,
        out_specs=(vmem,) * 4,
        scratch_shapes=scratch,
        compiler_params=pltpu.CompilerParams(
            collective_id=0, has_side_effects=True, vmem_limit_bytes=60 * 1024 * 1024),
        cost_estimate=pl.CostEstimate(
            flops=13_500_000_000, bytes_accessed=6_000_000, transcendentals=0),
        name="lora_projection",
    )(idx, ranks, tokens, weight, down_t, up_t, cotangent)
    return layer_out, input_grad, jnp.swapaxes(down_grad, 1, 2), jnp.swapaxes(up_grad, 1, 2)


def solution(mesh):
    return jax.shard_map(
        local,
        mesh=mesh,
        in_specs=(
            P("dp", "mp"),
            P("mp", "dp"),
            P("dp", "mp", None),
            P("dp", "mp", None),
            P("dp", "mp"),
            P(),
            P(),
        ),
        out_specs=(P("dp", "mp"), P("dp", "mp"), P("dp", "mp", None), P("dp", "mp", None)),
        check_vma=False,
    )
```

```python
import functools

import jax
import jax.numpy as jnp
from jax import lax
from jax.experimental import pallas as pl
from jax.experimental.pallas import tpu as pltpu
from jax.sharding import PartitionSpec as P

MESH = pl.DeviceIdType.MESH
BF = jnp.bfloat16
F32 = jnp.float32
NZ, NX, NY = 8, 4, 4
NT = (((1,), (1,)), ((), ()))


ORDER = (
    ("cot_out",), ("spread",), ("w_own", 0), ("tok_out",), ("own_copies",), ("one_hot",), ("cot_pass",),
    ("ring", 0, 1), ("select",), ("ring", 0, 2), ("w_own", 1), ("tok_pass",), ("ring", 0, 3),
    ("ring", 1, 1), ("ring", 0, 4), ("low",), ("bwd", 0), ("ring", 1, 2), ("low_sum",), ("fwd", 0),
    ("fwd", 1), ("ring", 1, 3), ("grads",), ("fwd", 2), ("ring", 1, 4), ("fwd", 3), ("fwd", 4), ("bwd", 1),
    ("tenant_sums",), ("sum_y",), ("grad_sums", 0), ("grad_result", 0), ("layer_result",),
    ("grad_sums", 1), ("grad_result", 1), ("factor_result",),
)


def kernel(
    idx, ranks, tok, w, dn, up, cot,
    o_y, o_g, o_dg, o_ug,
    fs, ft, ss, fac, gs, gr, sel, hs, hr, lp, lr, lo,
    wg, xg, cg, yp, yr, ys, yf, gp, gg, ge, gx,
    s_l, r_l, s_wa, r_wa, s_wb, r_wb, s_wc, r_wc, s_x, r_x, s_c, r_c, s_ca, r_ca,
    s_y, r_y, s_ya, r_ya, s_g, r_g, s_gx, r_gx, s_m, r_m, s_loc,
):
    dp = lax.axis_index("dp")
    mp = lax.axis_index("mp")
    z, x = dp // NX, dp % NX
    y, c = mp // 2, mp % 2
    o = 1 - c
    turn = 1 - 2 * c

    def dev(zz, xx, yy, cc):
        return (zz * NX + xx, yy * 2 + cc)

    def start(src, dst, s_sem, r_sem, device):
        copy = pltpu.make_async_remote_copy(
            src_ref=src, dst_ref=dst, send_sem=s_sem, recv_sem=r_sem,
            device_id=device, device_id_type=MESH,
        )
        copy.start()

    def wait(ref, sem):
        pltpu.make_async_copy(ref, ref, sem).wait()

    def ranks_at(i):
        return pl.ds(pl.multiple_of(16 * i, 16), 16)

    def lanes_at(i):
        return pl.ds(pl.multiple_of(256 * i, 256), 256)

    def half(i):
        return pl.ds(pl.multiple_of(192 * i, 192), 192)

    def dp_peer(k):
        return (z + k // NX) % NZ, (x + k % NX) % NX

    barrier = pltpu.get_barrier_semaphore()

    def greet_dp(k, carry):
        pz, px = dp_peer(k)
        pl.semaphore_signal(barrier, inc=1, device_id=dev(pz, px, y, c), device_id_type=MESH)
        return carry

    def greet_mp(k, carry):
        pl.semaphore_signal(barrier, inc=1, device_id=(dp, (mp + k) % 8), device_id_type=MESH)
        return carry

    def greet_x(k, carry):
        pl.semaphore_signal(barrier, inc=1, device_id=dev(z, (x + k) % NX, y, o), device_id_type=MESH)
        return carry

    lax.fori_loop(1, 32, greet_dp, 0)
    lax.fori_loop(1, 8, greet_mp, 0)
    lax.fori_loop(1, 4, greet_x, 0)

    for j in range(8):
        src = dn if j < 4 else up
        r0 = 16 * (j % 4)
        for i in range(4):
            fs[4 * j + i] = src[:, r0:r0 + 16, 256 * i:256 * i + 256]

    pl.semaphore_wait(barrier, 41)

    za, zb = (z + turn + NZ) % NZ, (z - turn + NZ) % NZ
    xr, xl = (x + 1) % NX, (x + 3) % NX
    met = set()

    def once(key, ref, sem):
        if key not in met:
            met.add(key)
            wait(ref, sem)

    def spread():
        def one(k, carry):
            pz, px = dp_peer(k)
            start(fs.at[pz * NX + px], ft.at[pl.ds(2 * dp, 2)], s_l.at[0], r_l.at[0], dev(pz, px, y, c))
            return carry

        lax.fori_loop(1, 32, one, 0)
        ft[pl.ds(2 * dp, 2)] = fs[dp]

    def w_own(j):
        rows = pl.ds(512 * j, 512)
        start(w.at[rows], wg.at[z, c, rows], s_wa.at[j, 0], r_wa.at[j, 0], dev(za, x, y, c))
        start(w.at[rows], wg.at[z, c, rows], s_wb.at[j, 0], r_wb.at[j, 0], dev(zb, x, y, c))
        start(w.at[rows], wg.at[z, c, rows], s_wc.at[j, 0], r_wc.at[j, 0], dev(z, x, y, o))

    def ring(j, k):
        rows = pl.ds(512 * j, 512)
        ca, cb = (z - turn * k + NZ) % NZ, (z + turn * k + NZ) % NZ
        a, b = wg.at[ca, c, rows], wg.at[cb, c, rows]
        wait(a, r_wa.at[j, k - 1])
        if k < 4:
            start(a, a, s_wa.at[j, k], r_wa.at[j, k], dev(za, x, y, c))
        start(a, a, s_wc.at[j, k], r_wc.at[j, k], dev(z, x, y, o))
        if k < 4:
            wait(b, r_wb.at[j, k - 1])
            if k < 3:
                start(b, b, s_wb.at[j, k], r_wb.at[j, k], dev(zb, x, y, c))
            start(b, b, s_wc.at[j, 4 + k], r_wc.at[j, 4 + k], dev(z, x, y, o))

    def need_core(j, k):
        once(("core", j, k), w.at[pl.ds(0, 512)], r_wc.at[j, k])

    def tok_out():
        for h in range(2):
            rows = tok.at[pl.ds(192 * h, 192)]
            start(rows, xg.at[c, x], s_x.at[h], r_x.at[c], dev(z, xr, y, h))
            start(rows, xg.at[c, x], s_x.at[2 + h], r_x.at[2 + c], dev(z, xl, y, h))
        start(tok.at[half(o)], xg.at[c, x], s_x.at[4], r_x.at[4], dev(z, x, y, o))

    def tok_pass():
        wait(xg.at[0, 0], r_x.at[0])
        start(xg.at[0, xl], xg.at[0, xl], s_x.at[5], r_x.at[5], dev(z, xr, y, c))
        wait(xg.at[0, 0], r_x.at[3])
        start(xg.at[1, xr], xg.at[1, xr], s_x.at[6], r_x.at[6], dev(z, xl, y, c))

    def need_tok():
        for j in (1, 2, 4, 5, 6):
            once(("tok", j), xg.at[0, 0], r_x.at[j])

    def cot_out():
        def one(j, carry):
            px, ph = (x + j // 2) % NX, (c + j % 2) % 2
            start(cot.at[half(ph), lanes_at(px)], cg.at[mp, x], s_c.at[j], r_c.at[j], dev(z, px, y, ph))
            return carry

        lax.fori_loop(1, 8, one, 0)

    def own_copies():
        copies = [
            pltpu.make_async_copy(w, wg.at[z, c], s_loc.at[0]),
            pltpu.make_async_copy(tok.at[half(c)], xg.at[c, x], s_loc.at[1]),
            pltpu.make_async_copy(cot.at[half(c), lanes_at(x)], cg.at[mp, x], s_loc.at[2]),
        ]
        for copy in copies:
            copy.start()
        for copy in copies:
            copy.wait()

    def cot_pass():
        for j in range(1, 8):
            wait(cg.at[0, 0], r_c.at[j])
        own = cg.at[pl.ds(2 * y, 2)]
        for d in (2, 1, 3):
            start(own, own, s_ca.at[d - 1], r_ca.at[d - 1], dev(z, x, (y + d) % NY, c))

    def need_cot():
        for d in range(3):
            once(("cot", d), cg.at[pl.ds(0, 2)], r_ca.at[d])

    def one_hot():
        lane = lax.broadcasted_iota(jnp.int32, (8, 1536), 1)

        def place(b, carry):
            return jnp.where(lane // 16 == b, idx[b] * 16 + lane % 16, carry)

        owner_row = lax.fori_loop(0, 96, place, jnp.zeros((8, 1536), jnp.int32))[0:1]

        def fill(i, carry):
            at = lax.broadcasted_iota(jnp.int32, (64, 1536), 0) + i * 64
            sel[pl.ds(pl.multiple_of(i * 64, 64), 64), :] = jnp.where(at == owner_row, 1.0, 0.0).astype(BF)
            return carry

        lax.fori_loop(0, 16, fill, 0)

    def forward(zc):
        acc = jnp.dot(xg[0].reshape(768, 1024), wg[zc, 0], preferred_element_type=F32)
        acc = acc + jnp.dot(xg[1].reshape(768, 1024), wg[zc, 1], preferred_element_type=F32)
        yp[zc] = acc.astype(BF)
        yd = zc // 2

        @pl.when(yd != y)
        def _():
            slot = ((y - yd + NY) % NY - 1) * 2 + zc % 2
            start(yp.at[zc], yr.at[slot], s_y.at[0], r_y.at[0], dev(z, x, yd, c))

    def fwd(k):
        need_tok()
        for j in range(2):
            need_core(j, k)
            if 0 < k < 4:
                need_core(j, 4 + k)
        if k in (0, 4):
            forward((z + k) % NZ)
        else:
            def one(i, carry):
                forward((z + (2 * i - 1) * turn * k + NZ) % NZ)
                return carry

            lax.fori_loop(0, 2, one, 0)

    def select():
        wait(ft.at[pl.ds(0, 62)], r_l.at[0])

        def one(k, carry):
            pz, px = dp_peer(k)
            p = pz * NX + px
            for s in range(3):
                ss[3 * p + s] = ft[idx[3 * p + s]]
            return carry

        lax.fori_loop(0, 32, one, 0)

        def send(k, carry):
            pz, px = dp_peer(k)
            start(ss.at[pl.ds(3 * (pz * NX + px), 3)], fac.at[:, ranks_at(z), lanes_at(x)],
                  s_l.at[1], r_l.at[1], dev(pz, px, y, c))
            return carry

        lax.fori_loop(1, 32, send, 0)
        own = pltpu.make_async_copy(
            ss.at[pl.ds(3 * dp, 3)], fac.at[:, ranks_at(z), lanes_at(x)], s_loc.at[0])
        own.start()
        own.wait()

    def piece(m):
        return pl.ds(pl.multiple_of(48 * m, 16), 48)

    def low():
        wait(ss.at[pl.ds(0, 93)], r_l.at[1])
        for s in range(3):
            rows = slice(128 * s, 128 * s + 128)
            a = lax.dot_general(tok[rows], fac[s, 0:64], NT, preferred_element_type=F32)
            b = lax.dot_general(cot[rows], fac[s, 64:128], NT, preferred_element_type=F32)
            lp[rows] = jnp.concatenate([a, b], axis=1)

        def send(k, carry):
            m = (mp + k) % 8
            start(lp.at[piece(m)], lr.at[mp], s_m.at[0], r_m.at[0], (dp, m))
            return carry

        lax.fori_loop(1, 8, send, 0)
        lr[mp] = lp[piece(mp)]

    def low_sum():
        wait(lr.at[pl.ds(0, 7)], r_m.at[0])
        total = lr[0]
        for m in range(1, 8):
            total = total + lr[m]
        rank_lane = lax.broadcasted_iota(jnp.int32, (16, 128), 1) % 64
        coefs = []
        for g in range(3):
            block = dp * 3 + (mp * 48 + 16 * g) // 128
            held = jnp.full((16, 128), ranks[idx[block]], jnp.int32)
            coefs.append(jnp.where(rank_lane < held, 16.0 / held.astype(F32), 0.0))
        lo[piece(mp)] = (total * jnp.concatenate(coefs, axis=0)).astype(BF)

        def send(k, carry):
            start(lo.at[piece(mp)], lo.at[piece(mp)], s_m.at[1], r_m.at[1], (dp, (mp + k) % 8))
            return carry

        lax.fori_loop(1, 8, send, 0)

    def grads():
        wait(lo.at[pl.ds(0, 336)], r_m.at[1])
        for s in range(3):
            rows = slice(128 * s, 128 * s + 128)
            turned = lo[rows].astype(F32).T.astype(BF)
            gs[s, 0:64] = jnp.dot(turned[64:128], tok[rows], preferred_element_type=F32).astype(BF)
            gs[s, 64:128] = jnp.dot(turned[0:64], cot[rows], preferred_element_type=F32).astype(BF)

        def send(k, carry):
            pz, px = dp_peer(k)
            start(gs.at[:, ranks_at(pz), lanes_at(px)], gr.at[pl.ds(3 * dp, 3)],
                  s_l.at[2], r_l.at[2], dev(pz, px, y, c))
            return carry

        lax.fori_loop(1, 32, send, 0)
        own = pltpu.make_async_copy(
            gs.at[:, ranks_at(z), lanes_at(x)], gr.at[pl.ds(3 * dp, 3)], s_loc.at[1])
        own.start()
        own.wait()

    def bwd(j):
        need_cot()
        for k in range(8):
            need_core(j, k)

        def one(i, carry):
            t = 4 * (i // 2) + 2 * j + i % 2
            acc = jnp.zeros((768, 256), F32)
            for n in range(8):
                acc = acc + lax.dot_general(
                    cg[n].reshape(768, 256), wg[n, i // 2, lanes_at(2 * j + i % 2), :], NT,
                    preferred_element_type=F32)
            gp[t] = acc.astype(BF).reshape(4, 192, 256)
            for d in (2, 1, 3):
                px = (x + d) % NX
                start(gp.at[t, px], gg.at[3 - d, t], s_g.at[d - 1], r_g.at[3 - d, t], dev(z, px, y, c))
            return carry

        lax.fori_loop(0, 4, one, 0)

    def sum_y():
        wait(yr, r_y.at[0])

        def one(i, carry):
            cc, px = i // 4, i % 4
            rows = pl.ds(pl.multiple_of(192 * px, 192), 192)
            acc = yp[2 * y + cc, rows].astype(F32)
            for d in range(3):
                acc = acc + yr[2 * d + cc, rows].astype(F32)
            ys[cc, px] = acc.astype(BF)
            return carry

        lax.fori_loop(0, 8, one, 0)

        def send(j, carry):
            px, pc = (x + j // 2) % NX, (c + j % 2) % 2
            start(ys.at[pc, px], yf.at[c, :, lanes_at(x)], s_ya.at[j], r_ya.at[j], dev(z, px, y, pc))
            return carry

        lax.fori_loop(1, 8, send, 0)
        own = pltpu.make_async_copy(ys.at[c, x], yf.at[c, :, lanes_at(x)], s_loc.at[2])
        own.start()
        own.wait()

    def tenant_sums():
        wait(gr.at[pl.ds(0, 93)], r_l.at[2])

        def one(i, carry):
            rows = pl.ds(pl.multiple_of(256 * i, 256), 256)
            acc = jnp.dot(sel[rows, :], gr[...].reshape(1536, 256), preferred_element_type=F32)
            hs[pl.ds(16 * i, 16)] = acc.astype(BF).reshape(16, 16, 256)
            return carry

        lax.fori_loop(0, 4, one, 0)

        def send(k, carry):
            pz, px = dp_peer(k)
            start(hs.at[pl.ds(2 * (pz * NX + px), 2)], hr.at[:, ranks_at(z), lanes_at(x)],
                  s_l.at[3], r_l.at[3], dev(pz, px, y, c))
            return carry

        lax.fori_loop(1, 32, send, 0)
        own = pltpu.make_async_copy(
            hs.at[pl.ds(2 * dp, 2)], hr.at[:, ranks_at(z), lanes_at(x)], s_loc.at[3])
        own.start()
        own.wait()

    def layer_result():
        for j in range(1, 8):
            wait(ys.at[0, 0], r_ya.at[j])
        for u in range(6):
            rows = slice(64 * u, 64 * u + 64)
            acc = jnp.dot(lo[rows, 0:64], fac[u // 2, 64:128], preferred_element_type=F32)
            part = slice(64 * (u % 3), 64 * (u % 3) + 64)
            o_y[rows] = (acc + yf[u // 3, part].astype(F32)).astype(BF)

    def sum_x(t):
        for d in range(3):
            wait(gg.at[0, 0], r_g.at[d, t])
        acc = gp[t, x].astype(F32)
        for d in range(3):
            acc = acc + gg[d, t].astype(F32)
        return acc

    def adapter_grad(h, i, q):
        rows = pl.ds(pl.multiple_of(192 * h + 64 * q, 64), 64)
        part = lo[rows, :][:, 64:128]
        return rows, jnp.dot(part, fac[(192 * h + 64 * q) // 128, 0:64, 256 * i:256 * i + 256],
                             preferred_element_type=F32)

    def grad_sums(j):
        for i in (2 * j, 2 * j + 1):
            ge[i] = sum_x(4 * o + i).astype(BF)
            start(ge.at[i], gx.at[i], s_gx.at[i], r_gx.at[i], dev(z, x, y, o))
        for i in (2 * j, 2 * j + 1):
            total = sum_x(4 * c + i)
            for q in range(3):
                rows, acc = adapter_grad(c, i, q)
                o_g[rows, 256 * i:256 * i + 256] = (acc + total[64 * q:64 * q + 64]).astype(BF)

    def grad_result(j):
        for i in (2 * j, 2 * j + 1):
            wait(ge.at[0], r_gx.at[i])
            for q in range(3):
                rows, acc = adapter_grad(o, i, q)
                part = gx[i, 64 * q:64 * q + 64].astype(F32)
                o_g[rows, 256 * i:256 * i + 256] = (acc + part).astype(BF)

    def factor_result():
        wait(hs.at[pl.ds(0, 62)], r_l.at[3])
        o_dg[...] = hr[:, 0:64].astype(F32)
        o_ug[...] = hr[:, 64:128].astype(F32)

    table = {
        "spread": spread,
        "w_own": w_own,
        "ring": ring,
        "tok_out": tok_out,
        "tok_pass": tok_pass,
        "cot_out": cot_out,
        "own_copies": own_copies,
        "cot_pass": cot_pass,
        "one_hot": one_hot,
        "fwd": fwd,
        "select": select,
        "low": low,
        "low_sum": low_sum,
        "grads": grads,
        "bwd": bwd,
        "sum_y": sum_y,
        "tenant_sums": tenant_sums,
        "layer_result": layer_result,
        "grad_sums": grad_sums,
        "grad_result": grad_result,
        "factor_result": factor_result,
    }
    for name, *at in ORDER:
        table[name](*at)

    wait(ft.at[pl.ds(0, 62)], s_l.at[0])
    wait(ss.at[pl.ds(0, 93)], s_l.at[1])
    wait(gr.at[pl.ds(0, 93)], s_l.at[2])
    wait(hs.at[pl.ds(0, 62)], s_l.at[3])
    wait(lr.at[pl.ds(0, 7)], s_m.at[0])
    wait(lo.at[pl.ds(0, 336)], s_m.at[1])
    for j in range(2):
        rows = w.at[pl.ds(0, 512)]
        for k in range(4):
            wait(rows, s_wa.at[j, k])
        for k in range(3):
            wait(rows, s_wb.at[j, k])
        for k in range(8):
            wait(rows, s_wc.at[j, k])
    for k in range(7):
        wait(xg.at[0, 0], s_x.at[k])
    for k in range(1, 8):
        wait(cg.at[0, 0], s_c.at[k])
        wait(ys.at[0, 0], s_ya.at[k])
    for d in range(3):
        wait(cg.at[pl.ds(0, 2)], s_ca.at[d])
        wait(gg.at[0], s_g.at[d])
    wait(yr, s_y.at[0])
    for i in range(4):
        wait(ge.at[0], s_gx.at[i])


def local(tokens, weight, down, up, cotangent, idx, ranks):
    down_t = jnp.swapaxes(down, 1, 2)
    up_t = jnp.swapaxes(up, 1, 2)
    vmem = pl.BlockSpec(memory_space=pltpu.VMEM)
    smem = pl.BlockSpec(memory_space=pltpu.SMEM)
    buf = lambda *shape: pltpu.VMEM(shape, BF)
    dma = lambda *shape: pltpu.SemaphoreType.DMA(shape)
    scratch = [
        buf(32, 2, 16, 256), buf(64, 16, 256), buf(96, 16, 256), buf(3, 128, 1024),
        buf(3, 128, 1024), buf(96, 16, 256), buf(1024, 1536), buf(64, 16, 256),
        buf(2, 128, 1024), pltpu.VMEM((384, 128), F32), pltpu.VMEM((8, 48, 128), F32),
        buf(384, 128),
        buf(8, 2, 1024, 256), buf(2, 4, 192, 1024), buf(8, 4, 192, 256),
        buf(8, 768, 256), buf(6, 768, 256), buf(2, 4, 192, 256), buf(2, 192, 1024),
        buf(8, 4, 192, 256), buf(3, 8, 192, 256), buf(4, 192, 256), buf(4, 192, 256),
        dma(4), dma(4), dma(2, 4), dma(2, 4), dma(2, 3), dma(2, 3), dma(2, 8), dma(2, 8), dma(7), dma(7),
        dma(8), dma(8), dma(3), dma(3),
        dma(1), dma(1), dma(8), dma(8), dma(3), dma(3, 8), dma(4), dma(4), dma(2), dma(2),
        dma(4),
    ]
    out = jax.ShapeDtypeStruct
    layer_out, input_grad, down_grad, up_grad = pl.pallas_call(
        kernel,
        out_shape=(
            out(tokens.shape, BF), out(cotangent.shape, BF),
            out(down_t.shape, F32), out(up_t.shape, F32),
        ),
        in_specs=[smem, smem] + [vmem] * 5,
        out_specs=(vmem,) * 4,
        scratch_shapes=scratch,
        compiler_params=pltpu.CompilerParams(
            collective_id=0, has_side_effects=True, vmem_limit_bytes=60 * 1024 * 1024),
        cost_estimate=pl.CostEstimate(
            flops=13_500_000_000, bytes_accessed=6_000_000, transcendentals=0),
        name="lora_projection",
    )(idx, ranks, tokens, weight, down_t, up_t, cotangent)
    return layer_out, input_grad, jnp.swapaxes(down_grad, 1, 2), jnp.swapaxes(up_grad, 1, 2)


def solution(mesh):
    return jax.shard_map(
        local,
        mesh=mesh,
        in_specs=(
            P("dp", "mp"),
            P("mp", "dp"),
            P("dp", "mp", None),
            P("dp", "mp", None),
            P("dp", "mp"),
            P(),
            P(),
        ),
        out_specs=(P("dp", "mp"), P("dp", "mp"), P("dp", "mp", None), P("dp", "mp", None)),
        check_vma=False,
    )
```

```python
import functools

import jax
import jax.numpy as jnp
from jax import lax
from jax.experimental import pallas as pl
from jax.experimental.pallas import tpu as pltpu
from jax.sharding import PartitionSpec as P

MESH = pl.DeviceIdType.MESH
BF = jnp.bfloat16
F32 = jnp.float32
NZ, NX, NY = 8, 4, 4
NT = (((1,), (1,)), ((), ()))


ORDER = (
    ("cot_out",), ("spread",), ("w_own", 0), ("tok_out",), ("own_copies",), ("one_hot",), ("cot_pass",),
    ("ring", 0, 1), ("select",), ("ring", 0, 2), ("w_own", 1), ("tok_pass",), ("cot_far",), ("ring", 0, 3),
    ("ring", 1, 1), ("ring", 0, 4), ("low",), ("bwd", 0), ("ring", 1, 2), ("low_sum",), ("bwd_far", 0),
    ("fwd", 0), ("fwd", 1), ("ring", 1, 3), ("grads",), ("fwd", 2), ("ring", 1, 4), ("fwd", 3), ("fwd", 4),
    ("bwd", 1), ("fwd_far", 0), ("fwd_far", 1), ("tenant_sums",), ("bwd_far", 1), ("sum_y",),
    ("grad_sums", 0), ("grad_result", 0), ("layer_result",), ("grad_sums", 1), ("grad_result", 1),
    ("factor_result",),
)


def kernel(
    idx, ranks, tok_in, w_in, dn_in, up_in, cot_in,
    y_out, g_out, dg_out, ug_out,
    fs, ft, ss, fac, gs, gr, sel, hs, hr, lp, lr, lo,
    wg, xg, cg, yp, yt, yr, ys, yf, gp, gt, gg, ge, gx,
    tok, w, dn, up, cot, o_y, o_g, o_dg, o_ug,
    s_l, r_l, s_wa, r_wa, s_wb, r_wb, s_wc, r_wc, s_x, r_x, s_c, r_c, s_ca, r_ca,
    s_y, r_y, r_yt, s_ya, r_ya, s_g, r_g, r_gt, s_gx, r_gx, s_m, r_m, s_loc, s_io,
):
    dp = lax.axis_index("dp")
    mp = lax.axis_index("mp")
    z, x = dp // NX, dp % NX
    y, c = mp // 2, mp % 2
    o = 1 - c
    turn = 1 - 2 * c

    def dev(zz, xx, yy, cc):
        return (zz * NX + xx, yy * 2 + cc)

    def start(src, dst, s_sem, r_sem, device):
        copy = pltpu.make_async_remote_copy(
            src_ref=src, dst_ref=dst, send_sem=s_sem, recv_sem=r_sem,
            device_id=device, device_id_type=MESH,
        )
        copy.start()

    def wait(ref, sem):
        pltpu.make_async_copy(ref, ref, sem).wait()

    def ranks_at(i):
        return pl.ds(pl.multiple_of(16 * i, 16), 16)

    def lanes_at(i):
        return pl.ds(pl.multiple_of(256 * i, 256), 256)

    def half(i):
        return pl.ds(pl.multiple_of(192 * i, 192), 192)

    def dp_peer(k):
        return (z + k // NX) % NZ, (x + k % NX) % NX

    loads = [
        pltpu.make_async_copy(a, b, s_io.at[i])
        for i, (a, b) in enumerate(((dn_in, dn), (up_in, up), (w_in, w), (cot_in, cot), (tok_in, tok)))
    ]
    for load in loads:
        load.start()

    barrier = pltpu.get_barrier_semaphore()

    def greet_dp(k, carry):
        pz, px = dp_peer(k)
        pl.semaphore_signal(barrier, inc=1, device_id=dev(pz, px, y, c), device_id_type=MESH)
        return carry

    def greet_mp(k, carry):
        pl.semaphore_signal(barrier, inc=1, device_id=(dp, (mp + k) % 8), device_id_type=MESH)
        return carry

    def greet_x(k, carry):
        pl.semaphore_signal(barrier, inc=1, device_id=dev(z, (x + k) % NX, y, o), device_id_type=MESH)
        return carry

    lax.fori_loop(1, 32, greet_dp, 0)
    lax.fori_loop(1, 8, greet_mp, 0)
    lax.fori_loop(1, 4, greet_x, 0)

    loads[0].wait()
    loads[1].wait()
    for j in range(8):
        src = dn if j < 4 else up
        r0 = 16 * (j % 4)
        for i in range(4):
            fs[4 * j + i] = src[:, r0:r0 + 16, 256 * i:256 * i + 256]

    for load in loads[2:]:
        load.wait()
    pl.semaphore_wait(barrier, 41)

    za, zb = (z + turn + NZ) % NZ, (z - turn + NZ) % NZ
    xr, xl = (x + 1) % NX, (x + 3) % NX
    yu, yl = (y + 1) % NY, (y + 3) % NY
    met = set()

    def once(key, ref, sem):
        if key not in met:
            met.add(key)
            wait(ref, sem)

    def spread():
        def one(k, carry):
            pz, px = dp_peer(k)
            start(fs.at[pz * NX + px], ft.at[pl.ds(2 * dp, 2)], s_l.at[0], r_l.at[0], dev(pz, px, y, c))
            return carry

        lax.fori_loop(1, 32, one, 0)
        ft[pl.ds(2 * dp, 2)] = fs[dp]

    def w_own(j):
        rows = pl.ds(512 * j, 512)
        start(w.at[rows], wg.at[z, c, rows], s_wa.at[j, 0], r_wa.at[j, 0], dev(za, x, y, c))
        start(w.at[rows], wg.at[z, c, rows], s_wb.at[j, 0], r_wb.at[j, 0], dev(zb, x, y, c))
        start(w.at[rows], wg.at[z, c, rows], s_wc.at[j, 0], r_wc.at[j, 0], dev(z, x, y, o))

    def ring(j, k):
        rows = pl.ds(512 * j, 512)
        ca, cb = (z - turn * k + NZ) % NZ, (z + turn * k + NZ) % NZ
        a, b = wg.at[ca, c, rows], wg.at[cb, c, rows]
        wait(a, r_wa.at[j, k - 1])
        if k < 4:
            start(a, a, s_wa.at[j, k], r_wa.at[j, k], dev(za, x, y, c))
        start(a, a, s_wc.at[j, k], r_wc.at[j, k], dev(z, x, y, o))
        if k < 4:
            wait(b, r_wb.at[j, k - 1])
            if k < 3:
                start(b, b, s_wb.at[j, k], r_wb.at[j, k], dev(zb, x, y, c))
            start(b, b, s_wc.at[j, 4 + k], r_wc.at[j, 4 + k], dev(z, x, y, o))

    def need_core(j, k):
        once(("core", j, k), w.at[pl.ds(0, 512)], r_wc.at[j, k])

    def tok_out():
        for h in range(2):
            rows = tok.at[pl.ds(192 * h, 192)]
            start(rows, xg.at[c, x], s_x.at[h], r_x.at[c], dev(z, xr, y, h))
            start(rows, xg.at[c, x], s_x.at[2 + h], r_x.at[2 + c], dev(z, xl, y, h))
        start(tok.at[half(o)], xg.at[c, x], s_x.at[4], r_x.at[4], dev(z, x, y, o))

    def tok_pass():
        wait(xg.at[0, 0], r_x.at[0])
        start(xg.at[0, xl], xg.at[0, xl], s_x.at[5], r_x.at[5], dev(z, xr, y, c))
        wait(xg.at[0, 0], r_x.at[3])
        start(xg.at[1, xr], xg.at[1, xr], s_x.at[6], r_x.at[6], dev(z, xl, y, c))

    def need_tok():
        for j in (1, 2, 4, 5, 6):
            once(("tok", j), xg.at[0, 0], r_x.at[j])

    def cot_out():
        def one(j, carry):
            px, ph = (x + j // 2) % NX, (c + j % 2) % 2
            start(cot.at[half(ph), lanes_at(px)], cg.at[mp, x], s_c.at[j], r_c.at[j], dev(z, px, y, ph))
            return carry

        lax.fori_loop(1, 8, one, 0)

    def own_copies():
        copies = [
            pltpu.make_async_copy(w, wg.at[z, c], s_loc.at[0]),
            pltpu.make_async_copy(tok.at[half(c)], xg.at[c, x], s_loc.at[1]),
            pltpu.make_async_copy(cot.at[half(c), lanes_at(x)], cg.at[mp, x], s_loc.at[2]),
        ]
        for copy in copies:
            copy.start()
        for copy in copies:
            copy.wait()

    def cot_pass():
        for j in range(1, 8):
            wait(cg.at[0, 0], r_c.at[j])
        for i in range(2):
            own = cg.at[2 * y + i]
            start(own, own, s_ca.at[i], r_ca.at[i], dev(z, x, yu, c))
            start(own, own, s_ca.at[2 + i], r_ca.at[2 + i], dev(z, x, yl, c))

    def cot_far():
        once(("cot", 0), cg.at[0], r_ca.at[0])
        start(cg.at[2 * yl], cg.at[2 * yl], s_ca.at[4], r_ca.at[4], dev(z, x, yu, c))
        once(("cot", 3), cg.at[0], r_ca.at[3])
        start(cg.at[2 * yu + 1], cg.at[2 * yu + 1], s_ca.at[5], r_ca.at[5], dev(z, x, yl, c))

    def need_cot():
        for d in range(6):
            once(("cot", d), cg.at[0], r_ca.at[d])

    def one_hot():
        lane = lax.broadcasted_iota(jnp.int32, (8, 1536), 1)

        def place(b, carry):
            return jnp.where(lane // 16 == b, idx[b] * 16 + lane % 16, carry)

        owner_row = lax.fori_loop(0, 96, place, jnp.zeros((8, 1536), jnp.int32))[0:1]

        def fill(i, carry):
            at = lax.broadcasted_iota(jnp.int32, (64, 1536), 0) + i * 64
            sel[pl.ds(pl.multiple_of(i * 64, 64), 64), :] = jnp.where(at == owner_row, 1.0, 0.0).astype(BF)
            return carry

        lax.fori_loop(0, 16, fill, 0)

    def forward(zc):
        acc = jnp.dot(xg[0].reshape(768, 1024), wg[zc, 0], preferred_element_type=F32)
        acc = acc + jnp.dot(xg[1].reshape(768, 1024), wg[zc, 1], preferred_element_type=F32)
        yp[zc] = acc.astype(BF)
        yd, par = zc // 2, zc % 2
        away = (y - yd + NY) % NY

        @pl.when(away == 2)
        def _():
            start(yp.at[zc], yt.at[par], s_y.at[2], r_yt.at[par], dev(z, x, (yd + 1 + 2 * par) % NY, c))

        @pl.when(away == 3 - 2 * par)
        def _():
            start(yp.at[zc], yr.at[2 + par], s_y.at[1], r_y.at[1], dev(z, x, yd, c))

    def fwd_far(par):
        wait(yt.at[0], r_yt.at[par])
        yd = (y + 3 - 2 * par) % NY
        zc = 2 * yd + par

        def one(i, carry):
            rows = pl.ds(pl.multiple_of(192 * i, 192), 192)
            yp[zc, rows] = (yp[zc, rows].astype(F32) + yt[par, rows].astype(F32)).astype(BF)
            return carry

        lax.fori_loop(0, 4, one, 0)
        start(yp.at[zc], yr.at[par], s_y.at[0], r_y.at[0], dev(z, x, yd, c))

    def fwd(k):
        need_tok()
        for j in range(2):
            need_core(j, k)
            if 0 < k < 4:
                need_core(j, 4 + k)
        if k in (0, 4):
            forward((z + k) % NZ)
        else:
            def one(i, carry):
                forward((z + (2 * i - 1) * turn * k + NZ) % NZ)
                return carry

            lax.fori_loop(0, 2, one, 0)

    def select():
        wait(ft.at[pl.ds(0, 62)], r_l.at[0])

        def one(k, carry):
            pz, px = dp_peer(k)
            p = pz * NX + px
            for s in range(3):
                ss[3 * p + s] = ft[idx[3 * p + s]]
            return carry

        lax.fori_loop(0, 32, one, 0)

        def send(k, carry):
            pz, px = dp_peer(k)
            start(ss.at[pl.ds(3 * (pz * NX + px), 3)], fac.at[:, ranks_at(z), lanes_at(x)],
                  s_l.at[1], r_l.at[1], dev(pz, px, y, c))
            return carry

        lax.fori_loop(1, 32, send, 0)
        own = pltpu.make_async_copy(
            ss.at[pl.ds(3 * dp, 3)], fac.at[:, ranks_at(z), lanes_at(x)], s_loc.at[0])
        own.start()
        own.wait()

    def piece(m):
        return pl.ds(pl.multiple_of(48 * m, 16), 48)

    def low():
        wait(ss.at[pl.ds(0, 93)], r_l.at[1])
        for s in range(3):
            rows = slice(128 * s, 128 * s + 128)
            a = lax.dot_general(tok[rows], fac[s, 0:64], NT, preferred_element_type=F32)
            b = lax.dot_general(cot[rows], fac[s, 64:128], NT, preferred_element_type=F32)
            lp[rows] = jnp.concatenate([a, b], axis=1)

        def send(k, carry):
            m = (mp + k) % 8
            start(lp.at[piece(m)], lr.at[mp], s_m.at[0], r_m.at[0], (dp, m))
            return carry

        lax.fori_loop(1, 8, send, 0)
        lr[mp] = lp[piece(mp)]

    def low_sum():
        wait(lr.at[pl.ds(0, 7)], r_m.at[0])
        total = lr[0]
        for m in range(1, 8):
            total = total + lr[m]
        rank_lane = lax.broadcasted_iota(jnp.int32, (16, 128), 1) % 64
        coefs = []
        for g in range(3):
            block = dp * 3 + (mp * 48 + 16 * g) // 128
            held = jnp.full((16, 128), ranks[idx[block]], jnp.int32)
            coefs.append(jnp.where(rank_lane < held, 16.0 / held.astype(F32), 0.0))
        lo[piece(mp)] = (total * jnp.concatenate(coefs, axis=0)).astype(BF)

        def send(k, carry):
            start(lo.at[piece(mp)], lo.at[piece(mp)], s_m.at[1], r_m.at[1], (dp, (mp + k) % 8))
            return carry

        lax.fori_loop(1, 8, send, 0)

    def grads():
        wait(lo.at[pl.ds(0, 336)], r_m.at[1])
        for s in range(3):
            rows = slice(128 * s, 128 * s + 128)
            turned = lo[rows].astype(F32).T.astype(BF)
            gs[s, 0:64] = jnp.dot(turned[64:128], tok[rows], preferred_element_type=F32).astype(BF)
            gs[s, 64:128] = jnp.dot(turned[0:64], cot[rows], preferred_element_type=F32).astype(BF)

        def send(k, carry):
            pz, px = dp_peer(k)
            start(gs.at[:, ranks_at(pz), lanes_at(px)], gr.at[pl.ds(3 * dp, 3)],
                  s_l.at[2], r_l.at[2], dev(pz, px, y, c))
            return carry

        lax.fori_loop(1, 32, send, 0)
        own = pltpu.make_async_copy(
            gs.at[:, ranks_at(z), lanes_at(x)], gr.at[pl.ds(3 * dp, 3)], s_loc.at[1])
        own.start()
        own.wait()

    def bwd(j):
        need_cot()
        for k in range(8):
            need_core(j, k)

        def one(i, carry):
            t = 4 * (i // 2) + 2 * j + i % 2
            acc = jnp.zeros((768, 256), F32)
            for n in range(8):
                acc = acc + lax.dot_general(
                    cg[n].reshape(768, 256), wg[n, i // 2, lanes_at(2 * j + i % 2), :], NT,
                    preferred_element_type=F32)
            gp[t] = acc.astype(BF).reshape(4, 192, 256)
            odd = i % 2
            ahead, back = (x + 1 + 2 * odd) % NX, (x + 3 - 2 * odd) % NX
            start(gp.at[t, (x + 2) % NX], gt.at[t], s_g.at[2], r_gt.at[t], dev(z, ahead, y, c))
            start(gp.at[t, back], gg.at[1, t], s_g.at[1], r_g.at[1, t], dev(z, back, y, c))
            return carry

        lax.fori_loop(0, 4, one, 0)

    def bwd_far(j):
        def one(i, carry):
            t = 4 * (i // 2) + 2 * j + i % 2
            ahead = (x + 1 + 2 * (i % 2)) % NX
            wait(gt.at[0], r_gt.at[t])
            gp[t, ahead] = (gp[t, ahead].astype(F32) + gt[t].astype(F32)).astype(BF)
            start(gp.at[t, ahead], gg.at[0, t], s_g.at[0], r_g.at[0, t], dev(z, ahead, y, c))
            return carry

        lax.fori_loop(0, 4, one, 0)

    def sum_y():
        wait(yr.at[pl.ds(0, 2)], r_y.at[0])
        wait(yr.at[pl.ds(2, 2)], r_y.at[1])

        def one(i, carry):
            cc, px = i // 4, i % 4
            rows = pl.ds(pl.multiple_of(192 * px, 192), 192)
            acc = yp[2 * y + cc, rows].astype(F32)
            for d in range(2):
                acc = acc + yr[2 * d + cc, rows].astype(F32)
            ys[cc, px] = acc.astype(BF)
            return carry

        lax.fori_loop(0, 8, one, 0)

        def send(j, carry):
            px, pc = (x + j // 2) % NX, (c + j % 2) % 2
            start(ys.at[pc, px], yf.at[c, :, lanes_at(x)], s_ya.at[j], r_ya.at[j], dev(z, px, y, pc))
            return carry

        lax.fori_loop(1, 8, send, 0)
        own = pltpu.make_async_copy(ys.at[c, x], yf.at[c, :, lanes_at(x)], s_loc.at[2])
        own.start()
        own.wait()

    def tenant_sums():
        wait(gr.at[pl.ds(0, 93)], r_l.at[2])

        def one(i, carry):
            rows = pl.ds(pl.multiple_of(256 * i, 256), 256)
            acc = jnp.dot(sel[rows, :], gr[...].reshape(1536, 256), preferred_element_type=F32)
            hs[pl.ds(16 * i, 16)] = acc.astype(BF).reshape(16, 16, 256)
            return carry

        lax.fori_loop(0, 4, one, 0)

        def send(k, carry):
            pz, px = dp_peer(k)
            start(hs.at[pl.ds(2 * (pz * NX + px), 2)], hr.at[:, ranks_at(z), lanes_at(x)],
                  s_l.at[3], r_l.at[3], dev(pz, px, y, c))
            return carry

        lax.fori_loop(1, 32, send, 0)
        own = pltpu.make_async_copy(
            hs.at[pl.ds(2 * dp, 2)], hr.at[:, ranks_at(z), lanes_at(x)], s_loc.at[3])
        own.start()
        own.wait()

    def layer_result():
        for j in range(1, 8):
            wait(ys.at[0, 0], r_ya.at[j])
        for u in range(6):
            rows = slice(64 * u, 64 * u + 64)
            acc = jnp.dot(lo[rows, 0:64], fac[u // 2, 64:128], preferred_element_type=F32)
            part = slice(64 * (u % 3), 64 * (u % 3) + 64)
            o_y[rows] = (acc + yf[u // 3, part].astype(F32)).astype(BF)
        pltpu.make_async_copy(o_y, y_out, s_io.at[5]).start()

    def sum_x(t):
        for d in range(2):
            wait(gg.at[0, 0], r_g.at[d, t])
        acc = gp[t, x].astype(F32)
        for d in range(2):
            acc = acc + gg[d, t].astype(F32)
        return acc

    def adapter_grad(h, i, q):
        rows = pl.ds(pl.multiple_of(192 * h + 64 * q, 64), 64)
        part = lo[rows, :][:, 64:128]
        return rows, jnp.dot(part, fac[(192 * h + 64 * q) // 128, 0:64, 256 * i:256 * i + 256],
                             preferred_element_type=F32)

    def grad_sums(j):
        for i in (2 * j, 2 * j + 1):
            ge[i] = sum_x(4 * o + i).astype(BF)
            start(ge.at[i], gx.at[i], s_gx.at[i], r_gx.at[i], dev(z, x, y, o))
        for i in (2 * j, 2 * j + 1):
            total = sum_x(4 * c + i)
            for q in range(3):
                rows, acc = adapter_grad(c, i, q)
                o_g[rows, 256 * i:256 * i + 256] = (acc + total[64 * q:64 * q + 64]).astype(BF)

    def grad_result(j):
        for i in (2 * j, 2 * j + 1):
            wait(ge.at[0], r_gx.at[i])
            for q in range(3):
                rows, acc = adapter_grad(o, i, q)
                part = gx[i, 64 * q:64 * q + 64].astype(F32)
                o_g[rows, 256 * i:256 * i + 256] = (acc + part).astype(BF)
        if j == 1:
            pltpu.make_async_copy(o_g, g_out, s_io.at[6]).start()

    def factor_result():
        wait(hs.at[pl.ds(0, 62)], r_l.at[3])
        o_dg[...] = hr[:, 0:64].astype(F32)
        pltpu.make_async_copy(o_dg, dg_out, s_io.at[7]).start()
        o_ug[...] = hr[:, 64:128].astype(F32)
        pltpu.make_async_copy(o_ug, ug_out, s_io.at[8]).start()

    table = {
        "spread": spread,
        "w_own": w_own,
        "ring": ring,
        "tok_out": tok_out,
        "tok_pass": tok_pass,
        "cot_out": cot_out,
        "own_copies": own_copies,
        "cot_pass": cot_pass,
        "one_hot": one_hot,
        "fwd": fwd,
        "fwd_far": fwd_far,
        "bwd_far": bwd_far,
        "cot_far": cot_far,
        "select": select,
        "low": low,
        "low_sum": low_sum,
        "grads": grads,
        "bwd": bwd,
        "sum_y": sum_y,
        "tenant_sums": tenant_sums,
        "layer_result": layer_result,
        "grad_sums": grad_sums,
        "grad_result": grad_result,
        "factor_result": factor_result,
    }
    for name, *at in ORDER:
        table[name](*at)

    for i, (a, b) in enumerate(((o_y, y_out), (o_g, g_out), (o_dg, dg_out), (o_ug, ug_out))):
        pltpu.make_async_copy(a, b, s_io.at[5 + i]).wait()

    wait(ft.at[pl.ds(0, 62)], s_l.at[0])
    wait(ss.at[pl.ds(0, 93)], s_l.at[1])
    wait(gr.at[pl.ds(0, 93)], s_l.at[2])
    wait(hs.at[pl.ds(0, 62)], s_l.at[3])
    wait(lr.at[pl.ds(0, 7)], s_m.at[0])
    wait(lo.at[pl.ds(0, 336)], s_m.at[1])
    for j in range(2):
        rows = w.at[pl.ds(0, 512)]
        for k in range(4):
            wait(rows, s_wa.at[j, k])
        for k in range(3):
            wait(rows, s_wb.at[j, k])
        for k in range(8):
            wait(rows, s_wc.at[j, k])
    for k in range(7):
        wait(xg.at[0, 0], s_x.at[k])
    for k in range(1, 8):
        wait(cg.at[0, 0], s_c.at[k])
        wait(ys.at[0, 0], s_ya.at[k])
    for d in range(6):
        wait(cg.at[0], s_ca.at[d])
    for d in range(2):
        wait(gg.at[0], s_g.at[d])
        wait(yr.at[pl.ds(0, 2)], s_y.at[d])
    wait(gt, s_g.at[2])
    wait(yt, s_y.at[2])
    for i in range(4):
        wait(ge.at[0], s_gx.at[i])


def hand_over(*refs):
    n = len(refs) // 2
    copies = [pltpu.make_async_copy(refs[i], refs[n + i], refs[-1].at[i]) for i in range(n)]
    for copy in copies:
        copy.start()
    for copy in copies:
        copy.wait()


def local(tokens, weight, down, up, cotangent, idx, ranks):
    down_t = jnp.swapaxes(down, 1, 2)
    up_t = jnp.swapaxes(up, 1, 2)
    anywhere = pl.BlockSpec(memory_space=pl.ANY)
    smem = pl.BlockSpec(memory_space=pltpu.SMEM)
    buf = lambda *shape: pltpu.VMEM(shape, BF)
    dma = lambda *shape: pltpu.SemaphoreType.DMA(shape)
    scratch = [
        buf(32, 2, 16, 256), buf(64, 16, 256), buf(96, 16, 256), buf(3, 128, 1024),
        buf(3, 128, 1024), buf(96, 16, 256), buf(1024, 1536), buf(64, 16, 256),
        buf(2, 128, 1024), pltpu.VMEM((384, 128), F32), pltpu.VMEM((8, 48, 128), F32),
        buf(384, 128),
        buf(8, 2, 1024, 256), buf(2, 4, 192, 1024), buf(8, 4, 192, 256),
        buf(8, 768, 256), buf(2, 768, 256), buf(4, 768, 256), buf(2, 4, 192, 256), buf(2, 192, 1024),
        buf(8, 4, 192, 256), buf(8, 192, 256), buf(2, 8, 192, 256), buf(4, 192, 256), buf(4, 192, 256),
        buf(384, 1024), buf(1024, 256), buf(2, 64, 1024), buf(2, 64, 1024), buf(384, 1024),
        buf(384, 1024), buf(384, 1024), pltpu.VMEM((2, 64, 1024), F32), pltpu.VMEM((2, 64, 1024), F32),
        dma(4), dma(4), dma(2, 4), dma(2, 4), dma(2, 3), dma(2, 3), dma(2, 8), dma(2, 8), dma(7), dma(7),
        dma(8), dma(8), dma(6), dma(6),
        dma(3), dma(2), dma(2), dma(8), dma(8), dma(3), dma(2, 8), dma(8), dma(4), dma(4), dma(2), dma(2),
        dma(4), dma(9),
    ]
    out = jax.ShapeDtypeStruct
    shapes = (
        out(tokens.shape, BF), out(cotangent.shape, BF), out(down_t.shape, F32), out(up_t.shape, F32),
    )
    results = pl.pallas_call(
        kernel,
        out_shape=shapes,
        in_specs=[smem, smem] + [anywhere] * 5,
        out_specs=(anywhere,) * 4,
        scratch_shapes=scratch,
        compiler_params=pltpu.CompilerParams(
            collective_id=0, has_side_effects=True, vmem_limit_bytes=60 * 1024 * 1024),
        cost_estimate=pl.CostEstimate(
            flops=13_500_000_000, bytes_accessed=6_000_000, transcendentals=0),
        name="lora_projection",
    )(idx, ranks, tokens, weight, down_t, up_t, cotangent)
    layer_out, input_grad, down_grad, up_grad = pl.pallas_call(
        hand_over,
        out_shape=shapes,
        in_specs=[anywhere] * 4,
        out_specs=(anywhere,) * 4,
        scratch_shapes=[dma(4)],
        name="hand_over",
    )(*results)
    return layer_out, input_grad, jnp.swapaxes(down_grad, 1, 2), jnp.swapaxes(up_grad, 1, 2)


def solution(mesh):
    return jax.shard_map(
        local,
        mesh=mesh,
        in_specs=(
            P("dp", "mp"),
            P("mp", "dp"),
            P("dp", "mp", None),
            P("dp", "mp", None),
            P("dp", "mp"),
            P(),
            P(),
        ),
        out_specs=(P("dp", "mp"), P("dp", "mp"), P("dp", "mp", None), P("dp", "mp", None)),
        check_vma=False,
    )
```

```python
import functools

import jax
import jax.numpy as jnp
from jax import lax
from jax.experimental import pallas as pl
from jax.experimental.pallas import tpu as pltpu
from jax.sharding import PartitionSpec as P

MESH = pl.DeviceIdType.MESH
BF = jnp.bfloat16
F32 = jnp.float32
NZ, NX, NY = 8, 4, 4
NT = (((1,), (1,)), ((), ()))


ORDER = (
    ("cot_out",), ("spread",), ("w_own", 0), ("w_own", 1), ("tok_out",), ("own_copies",), ("one_hot",),
    ("cot_pass",), ("ring", 0, 1), ("select",), ("ring", 1, 1), ("ring", 0, 2), ("tok_pass",),
    ("cot_far",), ("ring", 1, 2), ("fwd", 0), ("ring", 0, 3), ("fwd", 1), ("ring", 1, 3), ("ring", 0, 4),
    ("low",), ("bwd", 0), ("low_sum",), ("fwd", 2), ("ring", 1, 4), ("grads",), ("bwd_far", 0), ("fwd", 3),
    ("fwd", 4), ("bwd", 1), ("fwd_far", 0), ("fwd_far", 1), ("tenant_sums", 0), ("bwd_far", 1),
    ("tenant_sums", 1), ("sum_y",), ("grad_sums", 0), ("grad_result", 0), ("layer_result",),
    ("grad_sums", 1), ("grad_result", 1), ("factor_result",),
)


def kernel(
    idx, ranks, tok_in, w_in, dn_in, up_in, cot_in,
    y_out, g_out, dg_out, ug_out,
    fs, ft, ss, fac, gs, gr, sel, hs, hr, lp, lr, lo,
    wg, xg, cg, yp, yt, yr, ys, yf, gp, gt, gg, ge, gx,
    tok, w, dn, up, cot, o_y, o_g, o_dg, o_ug,
    s_l, r_l, s_wa, r_wa, s_wb, r_wb, s_wc, r_wc, s_x, r_x, s_c, r_c, s_ca, r_ca,
    s_y, r_y, r_yt, s_ya, r_ya, s_g, r_g, r_gt, s_gx, r_gx, s_m, r_m, s_loc, s_io,
):
    dp = lax.axis_index("dp")
    mp = lax.axis_index("mp")
    z, x = dp // NX, dp % NX
    y, c = mp // 2, mp % 2
    o = 1 - c
    turn = 1 - 2 * c

    def dev(zz, xx, yy, cc):
        return (zz * NX + xx, yy * 2 + cc)

    def start(src, dst, s_sem, r_sem, device):
        copy = pltpu.make_async_remote_copy(
            src_ref=src, dst_ref=dst, send_sem=s_sem, recv_sem=r_sem,
            device_id=device, device_id_type=MESH,
        )
        copy.start()

    def wait(ref, sem):
        pltpu.make_async_copy(ref, ref, sem).wait()

    def ranks_at(i):
        return pl.ds(pl.multiple_of(16 * i, 16), 16)

    def lanes_at(i):
        return pl.ds(pl.multiple_of(256 * i, 256), 256)

    def part_at(i, h):
        return pl.ds(pl.multiple_of(256 * i + 128 * h, 128), 128)

    def half(i):
        return pl.ds(pl.multiple_of(192 * i, 192), 192)

    xs = [x] + [lax.rem(x + d, NX) for d in range(1, NX)]

    def each_dp(act):
        for d in range(1, NX):
            act(z, xs[d])

        def one(d, carry):
            pz = lax.rem(z + d, NZ)
            for px in xs:
                act(pz, px)
            return carry

        lax.fori_loop(1, NZ, one, 0)

    loads = [
        pltpu.make_async_copy(a, b, s_io.at[i])
        for i, (a, b) in enumerate(((dn_in, dn), (up_in, up), (w_in, w), (cot_in, cot), (tok_in, tok)))
    ]
    for load in loads:
        load.start()

    barrier = pltpu.get_barrier_semaphore()

    def greet(device):
        pl.semaphore_signal(barrier, inc=1, device_id=device, device_id_type=MESH)

    each_dp(lambda pz, px: greet(dev(pz, px, y, c)))
    for k in range(1, 8):
        greet((dp, lax.rem(mp + k, 8)))
    for px in xs[1:]:
        greet(dev(z, px, y, o))

    loads[0].wait()
    loads[1].wait()
    for j in range(8):
        src = dn if j < 4 else up
        r0 = 16 * (j % 4)
        for i in range(4):
            fs[4 * j + i] = src[:, r0:r0 + 16, 256 * i:256 * i + 256]

    for load in loads[2:]:
        load.wait()
    pl.semaphore_wait(barrier, 41)

    za, zb = (z + turn + NZ) % NZ, (z - turn + NZ) % NZ
    xr, xl = (x + 1) % NX, (x + 3) % NX
    yu, yl = (y + 1) % NY, (y + 3) % NY
    met = set()

    def once(key, ref, sem):
        if key not in met:
            met.add(key)
            wait(ref, sem)

    def spread():
        def send(pz, px):
            start(fs.at[pz * NX + px], ft.at[pl.ds(2 * dp, 2)], s_l.at[0], r_l.at[0], dev(pz, px, y, c))

        each_dp(send)
        ft[pl.ds(2 * dp, 2)] = fs[dp]

    def w_own(j):
        rows = pl.ds(512 * j, 512)
        start(w.at[rows], wg.at[z, c, rows], s_wa.at[j, 0], r_wa.at[j, 0], dev(za, x, y, c))
        start(w.at[rows], wg.at[z, c, rows], s_wb.at[j, 0], r_wb.at[j, 0], dev(zb, x, y, c))
        start(w.at[rows], wg.at[z, c, rows], s_wc.at[j, 0], r_wc.at[j, 0], dev(z, x, y, o))

    def ring(j, k):
        rows = pl.ds(512 * j, 512)
        ca, cb = (z - turn * k + NZ) % NZ, (z + turn * k + NZ) % NZ
        a, b = wg.at[ca, c, rows], wg.at[cb, c, rows]
        wait(a, r_wa.at[j, k - 1])
        if k < 4:
            start(a, a, s_wa.at[j, k], r_wa.at[j, k], dev(za, x, y, c))
        start(a, a, s_wc.at[j, k], r_wc.at[j, k], dev(z, x, y, o))
        if k < 4:
            wait(b, r_wb.at[j, k - 1])
            if k < 3:
                start(b, b, s_wb.at[j, k], r_wb.at[j, k], dev(zb, x, y, c))
            start(b, b, s_wc.at[j, 4 + k], r_wc.at[j, 4 + k], dev(z, x, y, o))

    def need_core(j, k):
        once(("core", j, k), w.at[pl.ds(0, 512)], r_wc.at[j, k])

    def tok_out():
        for h in range(2):
            rows = tok.at[pl.ds(192 * h, 192)]
            start(rows, xg.at[c, x], s_x.at[h], r_x.at[c], dev(z, xr, y, h))
            start(rows, xg.at[c, x], s_x.at[2 + h], r_x.at[2 + c], dev(z, xl, y, h))
        start(tok.at[half(o)], xg.at[c, x], s_x.at[4], r_x.at[4], dev(z, x, y, o))

    def tok_pass():
        wait(xg.at[0, 0], r_x.at[0])
        start(xg.at[0, xl], xg.at[0, xl], s_x.at[5], r_x.at[5], dev(z, xr, y, c))
        wait(xg.at[0, 0], r_x.at[3])
        start(xg.at[1, xr], xg.at[1, xr], s_x.at[6], r_x.at[6], dev(z, xl, y, c))

    def need_tok():
        for j in (1, 2, 4, 5, 6):
            once(("tok", j), xg.at[0, 0], r_x.at[j])

    def cot_out():
        def one(j, carry):
            px, ph = (x + j // 2) % NX, (c + j % 2) % 2
            start(cot.at[half(ph), lanes_at(px)], cg.at[mp, x], s_c.at[j], r_c.at[j], dev(z, px, y, ph))
            return carry

        lax.fori_loop(1, 8, one, 0)

    def own_copies():
        copies = [
            pltpu.make_async_copy(w, wg.at[z, c], s_loc.at[0]),
            pltpu.make_async_copy(tok.at[half(c)], xg.at[c, x], s_loc.at[1]),
            pltpu.make_async_copy(cot.at[half(c), lanes_at(x)], cg.at[mp, x], s_loc.at[2]),
        ]
        for copy in copies:
            copy.start()
        for copy in copies:
            copy.wait()

    def cot_pass():
        for j in range(1, 8):
            wait(cg.at[0, 0], r_c.at[j])
        for i in range(2):
            own = cg.at[2 * y + i]
            start(own, own, s_ca.at[i], r_ca.at[i], dev(z, x, yu, c))
            start(own, own, s_ca.at[2 + i], r_ca.at[2 + i], dev(z, x, yl, c))

    def cot_far():
        once(("cot", 0), cg.at[0], r_ca.at[0])
        start(cg.at[2 * yl], cg.at[2 * yl], s_ca.at[4], r_ca.at[4], dev(z, x, yu, c))
        once(("cot", 3), cg.at[0], r_ca.at[3])
        start(cg.at[2 * yu + 1], cg.at[2 * yu + 1], s_ca.at[5], r_ca.at[5], dev(z, x, yl, c))

    def need_cot():
        for d in range(6):
            once(("cot", d), cg.at[0], r_ca.at[d])

    def one_hot():
        lane = lax.broadcasted_iota(jnp.int32, (8, 1536), 1)

        def place(b, carry):
            return jnp.where(lane // 16 == b, idx[b] * 16 + lane % 16, carry)

        owner_row = lax.fori_loop(0, 96, place, jnp.zeros((8, 1536), jnp.int32))[0:1]

        def fill(i, carry):
            at = lax.broadcasted_iota(jnp.int32, (64, 1536), 0) + i * 64
            sel[pl.ds(pl.multiple_of(i * 64, 64), 64), :] = jnp.where(at == owner_row, 1.0, 0.0).astype(BF)
            return carry

        lax.fori_loop(0, 16, fill, 0)

    def forward(zc):
        acc = jnp.dot(xg[0].reshape(768, 1024), wg[zc, 0], preferred_element_type=F32)
        acc = acc + jnp.dot(xg[1].reshape(768, 1024), wg[zc, 1], preferred_element_type=F32)
        yp[zc] = acc.astype(BF)
        yd, par = zc // 2, zc % 2
        away = (y - yd + NY) % NY

        @pl.when(away == 2)
        def _():
            start(yp.at[zc], yt.at[par], s_y.at[2], r_yt.at[par], dev(z, x, (yd + 1 + 2 * par) % NY, c))

        @pl.when(away == 3 - 2 * par)
        def _():
            start(yp.at[zc], yr.at[2 + par], s_y.at[1], r_y.at[1], dev(z, x, yd, c))

    def fwd_far(par):
        wait(yt.at[0], r_yt.at[par])
        yd = (y + 3 - 2 * par) % NY
        zc = 2 * yd + par

        def one(i, carry):
            rows = pl.ds(pl.multiple_of(192 * i, 192), 192)
            yp[zc, rows] = (yp[zc, rows].astype(F32) + yt[par, rows].astype(F32)).astype(BF)
            return carry

        lax.fori_loop(0, 4, one, 0)
        start(yp.at[zc], yr.at[par], s_y.at[0], r_y.at[0], dev(z, x, yd, c))

    def fwd(k):
        need_tok()
        for j in range(2):
            need_core(j, k)
            if 0 < k < 4:
                need_core(j, 4 + k)
        if k in (0, 4):
            forward((z + k) % NZ)
        else:
            def one(i, carry):
                forward((z + (2 * i - 1) * turn * k + NZ) % NZ)
                return carry

            lax.fori_loop(0, 2, one, 0)

    def select():
        wait(ft.at[pl.ds(0, 62)], r_l.at[0])

        def pick(p):
            for s in range(3):
                ss[3 * p + s] = ft[idx[3 * p + s]]

        def send(pz, px):
            p = pz * NX + px
            pick(p)
            start(ss.at[pl.ds(3 * p, 3)], fac.at[:, ranks_at(z), lanes_at(x)],
                  s_l.at[1], r_l.at[1], dev(pz, px, y, c))

        each_dp(send)
        pick(dp)
        own = pltpu.make_async_copy(
            ss.at[pl.ds(3 * dp, 3)], fac.at[:, ranks_at(z), lanes_at(x)], s_loc.at[0])
        own.start()
        own.wait()

    def piece(m):
        return pl.ds(pl.multiple_of(48 * m, 16), 48)

    def low():
        wait(ss.at[pl.ds(0, 93)], r_l.at[1])
        for s in range(3):
            rows = slice(128 * s, 128 * s + 128)
            a = lax.dot_general(tok[rows], fac[s, 0:64], NT, preferred_element_type=F32)
            b = lax.dot_general(cot[rows], fac[s, 64:128], NT, preferred_element_type=F32)
            lp[rows] = jnp.concatenate([a, b], axis=1)

        for k in range(1, 8):
            m = lax.rem(mp + k, 8)
            start(lp.at[piece(m)], lr.at[mp], s_m.at[0], r_m.at[0], (dp, m))
        lr[mp] = lp[piece(mp)]

    def low_sum():
        wait(lr.at[pl.ds(0, 7)], r_m.at[0])
        total = lr[0]
        for m in range(1, 8):
            total = total + lr[m]
        rank_lane = lax.broadcasted_iota(jnp.int32, (16, 128), 1) % 64
        coefs = []
        for g in range(3):
            block = dp * 3 + (mp * 48 + 16 * g) // 128
            held = jnp.full((16, 128), ranks[idx[block]], jnp.int32)
            coefs.append(jnp.where(rank_lane < held, 16.0 / held.astype(F32), 0.0))
        lo[piece(mp)] = (total * jnp.concatenate(coefs, axis=0)).astype(BF)

        for k in range(1, 8):
            start(lo.at[piece(mp)], lo.at[piece(mp)], s_m.at[1], r_m.at[1], (dp, lax.rem(mp + k, 8)))

    def grads():
        wait(lo.at[pl.ds(0, 336)], r_m.at[1])
        for s in range(3):
            rows = slice(128 * s, 128 * s + 128)
            turned = lo[rows].astype(F32).T.astype(BF)
            gs[s, 0:64] = jnp.dot(turned[64:128], tok[rows], preferred_element_type=F32).astype(BF)
            gs[s, 64:128] = jnp.dot(turned[0:64], cot[rows], preferred_element_type=F32).astype(BF)

        for h in range(2):
            def send(pz, px):
                start(gs.at[:, ranks_at(pz), part_at(px, h)], gr.at[h, pl.ds(3 * dp, 3)],
                      s_l.at[2 + h], r_l.at[2 + h], dev(pz, px, y, c))

            each_dp(send)
        for h in range(2):
            own = pltpu.make_async_copy(
                gs.at[:, ranks_at(z), part_at(x, h)], gr.at[h, pl.ds(3 * dp, 3)], s_loc.at[1])
            own.start()
            own.wait()

    def bwd(j):
        need_cot()
        for k in range(8):
            need_core(j, k)

        def one(i, carry):
            t = 4 * (i // 2) + 2 * j + i % 2
            acc = jnp.zeros((768, 256), F32)
            for n in range(8):
                acc = acc + lax.dot_general(
                    cg[n].reshape(768, 256), wg[n, i // 2, lanes_at(2 * j + i % 2), :], NT,
                    preferred_element_type=F32)
            gp[t] = acc.astype(BF).reshape(4, 192, 256)
            odd = i % 2
            ahead, back = (x + 1 + 2 * odd) % NX, (x + 3 - 2 * odd) % NX
            start(gp.at[t, (x + 2) % NX], gt.at[t], s_g.at[2], r_gt.at[t], dev(z, ahead, y, c))
            start(gp.at[t, back], gg.at[1, t], s_g.at[1], r_g.at[1, t], dev(z, back, y, c))
            return carry

        lax.fori_loop(0, 4, one, 0)

    def bwd_far(j):
        def one(i, carry):
            t = 4 * (i // 2) + 2 * j + i % 2
            ahead = (x + 1 + 2 * (i % 2)) % NX
            wait(gt.at[0], r_gt.at[t])
            gp[t, ahead] = (gp[t, ahead].astype(F32) + gt[t].astype(F32)).astype(BF)
            start(gp.at[t, ahead], gg.at[0, t], s_g.at[0], r_g.at[0, t], dev(z, ahead, y, c))
            return carry

        lax.fori_loop(0, 4, one, 0)

    def sum_y():
        wait(yr.at[pl.ds(0, 2)], r_y.at[0])
        wait(yr.at[pl.ds(2, 2)], r_y.at[1])

        def one(i, carry):
            cc, px = i // 4, i % 4
            rows = pl.ds(pl.multiple_of(192 * px, 192), 192)
            acc = yp[2 * y + cc, rows].astype(F32)
            for d in range(2):
                acc = acc + yr[2 * d + cc, rows].astype(F32)
            ys[cc, px] = acc.astype(BF)
            return carry

        lax.fori_loop(0, 8, one, 0)

        def send(j, carry):
            px, pc = (x + j // 2) % NX, (c + j % 2) % 2
            start(ys.at[pc, px], yf.at[c, :, lanes_at(x)], s_ya.at[j], r_ya.at[j], dev(z, px, y, pc))
            return carry

        lax.fori_loop(1, 8, send, 0)
        own = pltpu.make_async_copy(ys.at[c, x], yf.at[c, :, lanes_at(x)], s_loc.at[2])
        own.start()
        own.wait()

    def tenant_sums(h):
        wait(gr.at[h, pl.ds(0, 93)], r_l.at[2 + h])

        def one(i, carry):
            rows = pl.ds(pl.multiple_of(256 * i, 256), 256)
            acc = jnp.dot(sel[rows, :], gr[h].reshape(1536, 128), preferred_element_type=F32)
            hs[h, pl.ds(16 * i, 16)] = acc.astype(BF).reshape(16, 16, 128)
            return carry

        lax.fori_loop(0, 4, one, 0)

        def send(pz, px):
            start(hs.at[h, pl.ds(2 * (pz * NX + px), 2)], hr.at[:, ranks_at(z), part_at(x, h)],
                  s_l.at[4 + h], r_l.at[4 + h], dev(pz, px, y, c))

        each_dp(send)
        own = pltpu.make_async_copy(
            hs.at[h, pl.ds(2 * dp, 2)], hr.at[:, ranks_at(z), part_at(x, h)], s_loc.at[3])
        own.start()
        own.wait()

    def layer_result():
        for j in range(1, 8):
            wait(ys.at[0, 0], r_ya.at[j])
        for u in range(6):
            rows = slice(64 * u, 64 * u + 64)
            acc = jnp.dot(lo[rows, 0:64], fac[u // 2, 64:128], preferred_element_type=F32)
            part = slice(64 * (u % 3), 64 * (u % 3) + 64)
            o_y[rows] = (acc + yf[u // 3, part].astype(F32)).astype(BF)
        pltpu.make_async_copy(o_y, y_out, s_io.at[5]).start()

    def sum_x(t):
        for d in range(2):
            wait(gg.at[0, 0], r_g.at[d, t])
        acc = gp[t, x].astype(F32)
        for d in range(2):
            acc = acc + gg[d, t].astype(F32)
        return acc

    def adapter_grad(h, i, q):
        rows = pl.ds(pl.multiple_of(192 * h + 64 * q, 64), 64)
        part = lo[rows, :][:, 64:128]
        return rows, jnp.dot(part, fac[(192 * h + 64 * q) // 128, 0:64, 256 * i:256 * i + 256],
                             preferred_element_type=F32)

    def grad_sums(j):
        for i in (2 * j, 2 * j + 1):
            ge[i] = sum_x(4 * o + i).astype(BF)
            start(ge.at[i], gx.at[i], s_gx.at[i], r_gx.at[i], dev(z, x, y, o))
        for i in (2 * j, 2 * j + 1):
            total = sum_x(4 * c + i)
            for q in range(3):
                rows, acc = adapter_grad(c, i, q)
                o_g[rows, 256 * i:256 * i + 256] = (acc + total[64 * q:64 * q + 64]).astype(BF)

    def grad_result(j):
        for i in (2 * j, 2 * j + 1):
            wait(ge.at[0], r_gx.at[i])
            for q in range(3):
                rows, acc = adapter_grad(o, i, q)
                part = gx[i, 64 * q:64 * q + 64].astype(F32)
                o_g[rows, 256 * i:256 * i + 256] = (acc + part).astype(BF)
        if j == 1:
            pltpu.make_async_copy(o_g, g_out, s_io.at[6]).start()

    def factor_result():
        for h in range(2):
            wait(hs.at[h, pl.ds(0, 62)], r_l.at[4 + h])
        o_dg[...] = hr[:, 0:64].astype(F32)
        pltpu.make_async_copy(o_dg, dg_out, s_io.at[7]).start()
        o_ug[...] = hr[:, 64:128].astype(F32)
        pltpu.make_async_copy(o_ug, ug_out, s_io.at[8]).start()

    table = {
        "spread": spread,
        "w_own": w_own,
        "ring": ring,
        "tok_out": tok_out,
        "tok_pass": tok_pass,
        "cot_out": cot_out,
        "own_copies": own_copies,
        "cot_pass": cot_pass,
        "one_hot": one_hot,
        "fwd": fwd,
        "fwd_far": fwd_far,
        "bwd_far": bwd_far,
        "cot_far": cot_far,
        "select": select,
        "low": low,
        "low_sum": low_sum,
        "grads": grads,
        "bwd": bwd,
        "sum_y": sum_y,
        "tenant_sums": tenant_sums,
        "layer_result": layer_result,
        "grad_sums": grad_sums,
        "grad_result": grad_result,
        "factor_result": factor_result,
    }
    for name, *at in ORDER:
        table[name](*at)

    for i, (a, b) in enumerate(((o_y, y_out), (o_g, g_out), (o_dg, dg_out), (o_ug, ug_out))):
        pltpu.make_async_copy(a, b, s_io.at[5 + i]).wait()

    wait(ft.at[pl.ds(0, 62)], s_l.at[0])
    wait(ss.at[pl.ds(0, 93)], s_l.at[1])
    for h in range(2):
        wait(gr.at[h, pl.ds(0, 93)], s_l.at[2 + h])
        wait(hs.at[h, pl.ds(0, 62)], s_l.at[4 + h])
    wait(lr.at[pl.ds(0, 7)], s_m.at[0])
    wait(lo.at[pl.ds(0, 336)], s_m.at[1])
    for j in range(2):
        rows = w.at[pl.ds(0, 512)]
        for k in range(4):
            wait(rows, s_wa.at[j, k])
        for k in range(3):
            wait(rows, s_wb.at[j, k])
        for k in range(8):
            wait(rows, s_wc.at[j, k])
    for k in range(7):
        wait(xg.at[0, 0], s_x.at[k])
    for k in range(1, 8):
        wait(cg.at[0, 0], s_c.at[k])
        wait(ys.at[0, 0], s_ya.at[k])
    for d in range(6):
        wait(cg.at[0], s_ca.at[d])
    for d in range(2):
        wait(gg.at[0], s_g.at[d])
        wait(yr.at[pl.ds(0, 2)], s_y.at[d])
    wait(gt, s_g.at[2])
    wait(yt, s_y.at[2])
    for i in range(4):
        wait(ge.at[0], s_gx.at[i])


def hand_over(*refs):
    held, arrived, left = refs[8:12], refs[12], refs[13]
    inward = [pltpu.make_async_copy(refs[i], held[i], arrived.at[i]) for i in range(4)]
    outward = [pltpu.make_async_copy(held[i], refs[4 + i], left.at[i]) for i in range(4)]
    for copy in inward:
        copy.start()
    for i in range(4):
        inward[i].wait()
        outward[i].start()
    for copy in outward:
        copy.wait()


def local(tokens, weight, down, up, cotangent, idx, ranks):
    down_t = jnp.swapaxes(down, 1, 2)
    up_t = jnp.swapaxes(up, 1, 2)
    anywhere = pl.BlockSpec(memory_space=pl.ANY)
    smem = pl.BlockSpec(memory_space=pltpu.SMEM)
    buf = lambda *shape: pltpu.VMEM(shape, BF)
    dma = lambda *shape: pltpu.SemaphoreType.DMA(shape)
    scratch = [
        buf(32, 2, 16, 256), buf(64, 16, 256), buf(96, 16, 256), buf(3, 128, 1024),
        buf(3, 128, 1024), buf(2, 96, 16, 128), buf(1024, 1536), buf(2, 64, 16, 128),
        buf(2, 128, 1024), pltpu.VMEM((384, 128), F32), pltpu.VMEM((8, 48, 128), F32),
        buf(384, 128),
        buf(8, 2, 1024, 256), buf(2, 4, 192, 1024), buf(8, 4, 192, 256),
        buf(8, 768, 256), buf(2, 768, 256), buf(4, 768, 256), buf(2, 4, 192, 256), buf(2, 192, 1024),
        buf(8, 4, 192, 256), buf(8, 192, 256), buf(2, 8, 192, 256), buf(4, 192, 256), buf(4, 192, 256),
        buf(384, 1024), buf(1024, 256), buf(2, 64, 1024), buf(2, 64, 1024), buf(384, 1024),
        buf(384, 1024), buf(384, 1024), pltpu.VMEM((2, 64, 1024), F32), pltpu.VMEM((2, 64, 1024), F32),
        dma(6), dma(6), dma(2, 4), dma(2, 4), dma(2, 3), dma(2, 3), dma(2, 8), dma(2, 8), dma(7), dma(7),
        dma(8), dma(8), dma(6), dma(6),
        dma(3), dma(2), dma(2), dma(8), dma(8), dma(3), dma(2, 8), dma(8), dma(4), dma(4), dma(2), dma(2),
        dma(4), dma(9),
    ]
    out = jax.ShapeDtypeStruct
    shapes = (
        out(tokens.shape, BF), out(cotangent.shape, BF), out(down_t.shape, F32), out(up_t.shape, F32),
    )
    results = pl.pallas_call(
        kernel,
        out_shape=shapes,
        in_specs=[smem, smem] + [anywhere] * 5,
        out_specs=(anywhere,) * 4,
        scratch_shapes=scratch,
        compiler_params=pltpu.CompilerParams(
            collective_id=0, has_side_effects=True, vmem_limit_bytes=60 * 1024 * 1024),
        cost_estimate=pl.CostEstimate(
            flops=13_500_000_000, bytes_accessed=6_000_000, transcendentals=0),
        name="lora_projection",
    )(idx, ranks, tokens, weight, down_t, up_t, cotangent)
    layer_out, input_grad, down_grad, up_grad = pl.pallas_call(
        hand_over,
        out_shape=shapes,
        in_specs=[anywhere] * 4,
        out_specs=(anywhere,) * 4,
        scratch_shapes=[pltpu.VMEM(a.shape, a.dtype) for a in shapes] + [dma(4), dma(4)],
        name="hand_over",
    )(*results)
    return layer_out, input_grad, jnp.swapaxes(down_grad, 1, 2), jnp.swapaxes(up_grad, 1, 2)


def solution(mesh):
    return jax.shard_map(
        local,
        mesh=mesh,
        in_specs=(
            P("dp", "mp"),
            P("mp", "dp"),
            P("dp", "mp", None),
            P("dp", "mp", None),
            P("dp", "mp"),
            P(),
            P(),
        ),
        out_specs=(P("dp", "mp"), P("dp", "mp"), P("dp", "mp", None), P("dp", "mp", None)),
        check_vma=False,
    )
```

```python
import functools

import jax
import jax.numpy as jnp
from jax import lax
from jax.experimental import pallas as pl
from jax.experimental.pallas import tpu as pltpu
from jax.sharding import PartitionSpec as P

MESH = pl.DeviceIdType.MESH
BF = jnp.bfloat16
F32 = jnp.float32
NZ, NX, NY = 8, 4, 4
NT = (((1,), (1,)), ((), ()))


ORDER = (
    ("cot_out",), ("spread",), ("w_own", 0), ("w_own", 1), ("tok_out",), ("own_copies",), ("one_hot",),
    ("cot_pass",), ("ring", 0, 1), ("select",), ("ring", 1, 1), ("ring", 0, 2), ("tok_pass",),
    ("cot_far",), ("ring", 1, 2), ("fwd", 0), ("ring", 0, 3), ("fwd", 1), ("ring", 1, 3), ("ring", 0, 4),
    ("low",), ("bwd", 0), ("low_sum",), ("fwd", 2), ("ring", 1, 4), ("grads",), ("bwd_far", 0), ("fwd", 3),
    ("fwd", 4), ("bwd", 1), ("fwd_far", 0), ("fwd_far", 1), ("tenant_sums", 0), ("bwd_far", 1), ("sum_y",),
    ("tenant_sums", 1), ("grad_sums", 0), ("grad_result", 0), ("layer_result",), ("grad_sums", 1),
    ("grad_result", 1), ("factor_result",),
)


def kernel(
    idx, ranks, tok_in, w_in, dn_in, up_in, cot_in,
    y_out, g_out, f_out,
    fs, ft, ss, fac, gs, gr, sel, hs, hr, lp, lr, lo,
    wg, xg, cg, yp, yt, yr, ys, yf, gp, gt, gg, ge, gx,
    tok, w, dn, up, cot, o_y, o_g,
    s_l, r_l, s_wa, r_wa, s_wb, r_wb, s_wc, r_wc, s_x, r_x, s_c, r_c, s_ca, r_ca,
    s_y, r_y, r_yt, s_ya, r_ya, s_g, r_g, r_gt, s_gx, r_gx, s_m, r_m, s_loc, s_io,
):
    dp = lax.axis_index("dp")
    mp = lax.axis_index("mp")
    z, x = dp // NX, dp % NX
    y, c = mp // 2, mp % 2
    o = 1 - c
    turn = 1 - 2 * c

    def dev(zz, xx, yy, cc):
        return (zz * NX + xx, yy * 2 + cc)

    def start(src, dst, s_sem, r_sem, device):
        copy = pltpu.make_async_remote_copy(
            src_ref=src, dst_ref=dst, send_sem=s_sem, recv_sem=r_sem,
            device_id=device, device_id_type=MESH,
        )
        copy.start()

    def wait(ref, sem):
        pltpu.make_async_copy(ref, ref, sem).wait()

    def ranks_at(i):
        return pl.ds(pl.multiple_of(16 * i, 16), 16)

    def lanes_at(i):
        return pl.ds(pl.multiple_of(256 * i, 256), 256)

    def part_at(i, h):
        return pl.ds(pl.multiple_of(256 * i + 128 * h, 128), 128)

    def half(i):
        return pl.ds(pl.multiple_of(192 * i, 192), 192)

    xs = [x] + [lax.rem(x + d, NX) for d in range(1, NX)]

    def each_dp(act):
        for d in range(1, NX):
            act(z, xs[d])

        def one(d, carry):
            pz = lax.rem(z + d, NZ)
            for px in xs:
                act(pz, px)
            return carry

        lax.fori_loop(1, NZ, one, 0)

    loads = [
        pltpu.make_async_copy(a, b, s_io.at[i])
        for i, (a, b) in enumerate(((dn_in, dn), (up_in, up), (w_in, w), (cot_in, cot), (tok_in, tok)))
    ]
    for load in loads:
        load.start()

    barrier = pltpu.get_barrier_semaphore()

    def greet(device):
        pl.semaphore_signal(barrier, inc=1, device_id=device, device_id_type=MESH)

    each_dp(lambda pz, px: greet(dev(pz, px, y, c)))
    for k in range(1, 8):
        greet((dp, lax.rem(mp + k, 8)))
    for px in xs[1:]:
        greet(dev(z, px, y, o))

    loads[0].wait()
    loads[1].wait()
    for j in range(8):
        src = dn if j < 4 else up
        r0 = 16 * (j % 4)
        for i in range(4):
            fs[4 * j + i] = src[:, r0:r0 + 16, 256 * i:256 * i + 256]

    for load in loads[2:]:
        load.wait()
    pl.semaphore_wait(barrier, 41)

    za, zb = (z + turn + NZ) % NZ, (z - turn + NZ) % NZ
    xr, xl = (x + 1) % NX, (x + 3) % NX
    yu, yl = (y + 1) % NY, (y + 3) % NY
    met = set()

    def once(key, ref, sem):
        if key not in met:
            met.add(key)
            wait(ref, sem)

    def spread():
        def send(pz, px):
            start(fs.at[pz * NX + px], ft.at[pl.ds(2 * dp, 2)], s_l.at[0], r_l.at[0], dev(pz, px, y, c))

        each_dp(send)
        ft[pl.ds(2 * dp, 2)] = fs[dp]

    def w_own(j):
        rows = pl.ds(512 * j, 512)
        start(w.at[rows], wg.at[z, c, rows], s_wa.at[j, 0], r_wa.at[j, 0], dev(za, x, y, c))
        start(w.at[rows], wg.at[z, c, rows], s_wb.at[j, 0], r_wb.at[j, 0], dev(zb, x, y, c))
        start(w.at[rows], wg.at[z, c, rows], s_wc.at[j, 0], r_wc.at[j, 0], dev(z, x, y, o))

    def ring(j, k):
        rows = pl.ds(512 * j, 512)
        ca, cb = (z - turn * k + NZ) % NZ, (z + turn * k + NZ) % NZ
        a, b = wg.at[ca, c, rows], wg.at[cb, c, rows]
        wait(a, r_wa.at[j, k - 1])
        if k < 4:
            start(a, a, s_wa.at[j, k], r_wa.at[j, k], dev(za, x, y, c))
        start(a, a, s_wc.at[j, k], r_wc.at[j, k], dev(z, x, y, o))
        if k < 4:
            wait(b, r_wb.at[j, k - 1])
            if k < 3:
                start(b, b, s_wb.at[j, k], r_wb.at[j, k], dev(zb, x, y, c))
            start(b, b, s_wc.at[j, 4 + k], r_wc.at[j, 4 + k], dev(z, x, y, o))

    def need_core(j, k):
        once(("core", j, k), w.at[pl.ds(0, 512)], r_wc.at[j, k])

    def tok_out():
        for h in range(2):
            rows = tok.at[pl.ds(192 * h, 192)]
            start(rows, xg.at[c, x], s_x.at[h], r_x.at[c], dev(z, xr, y, h))
            start(rows, xg.at[c, x], s_x.at[2 + h], r_x.at[2 + c], dev(z, xl, y, h))
        start(tok.at[half(o)], xg.at[c, x], s_x.at[4], r_x.at[4], dev(z, x, y, o))

    def tok_pass():
        wait(xg.at[0, 0], r_x.at[0])
        start(xg.at[0, xl], xg.at[0, xl], s_x.at[5], r_x.at[5], dev(z, xr, y, c))
        wait(xg.at[0, 0], r_x.at[3])
        start(xg.at[1, xr], xg.at[1, xr], s_x.at[6], r_x.at[6], dev(z, xl, y, c))

    def need_tok():
        for j in (1, 2, 4, 5, 6):
            once(("tok", j), xg.at[0, 0], r_x.at[j])

    def cot_out():
        def one(j, carry):
            px, ph = (x + j // 2) % NX, (c + j % 2) % 2
            start(cot.at[half(ph), lanes_at(px)], cg.at[mp, x], s_c.at[j], r_c.at[j], dev(z, px, y, ph))
            return carry

        lax.fori_loop(1, 8, one, 0)

    def own_copies():
        copies = [
            pltpu.make_async_copy(w, wg.at[z, c], s_loc.at[0]),
            pltpu.make_async_copy(tok.at[half(c)], xg.at[c, x], s_loc.at[1]),
            pltpu.make_async_copy(cot.at[half(c), lanes_at(x)], cg.at[mp, x], s_loc.at[2]),
        ]
        for copy in copies:
            copy.start()
        for copy in copies:
            copy.wait()

    def cot_pass():
        for j in range(1, 8):
            wait(cg.at[0, 0], r_c.at[j])
        for i in range(2):
            own = cg.at[2 * y + i]
            start(own, own, s_ca.at[i], r_ca.at[i], dev(z, x, yu, c))
            start(own, own, s_ca.at[2 + i], r_ca.at[2 + i], dev(z, x, yl, c))

    def cot_far():
        once(("cot", 0), cg.at[0], r_ca.at[0])
        start(cg.at[2 * yl], cg.at[2 * yl], s_ca.at[4], r_ca.at[4], dev(z, x, yu, c))
        once(("cot", 3), cg.at[0], r_ca.at[3])
        start(cg.at[2 * yu + 1], cg.at[2 * yu + 1], s_ca.at[5], r_ca.at[5], dev(z, x, yl, c))

    def need_cot():
        for d in range(6):
            once(("cot", d), cg.at[0], r_ca.at[d])

    def one_hot():
        lane = lax.broadcasted_iota(jnp.int32, (8, 1536), 1)

        def place(b, carry):
            return jnp.where(lane // 16 == b, idx[b] * 16 + lane % 16, carry)

        owner_row = lax.fori_loop(0, 96, place, jnp.zeros((8, 1536), jnp.int32))[0:1]

        def fill(i, carry):
            at = lax.broadcasted_iota(jnp.int32, (64, 1536), 0) + i * 64
            sel[pl.ds(pl.multiple_of(i * 64, 64), 64), :] = jnp.where(at == owner_row, 1.0, 0.0).astype(BF)
            return carry

        lax.fori_loop(0, 16, fill, 0)

    def forward(zc):
        acc = jnp.dot(xg[0].reshape(768, 1024), wg[zc, 0], preferred_element_type=F32)
        acc = acc + jnp.dot(xg[1].reshape(768, 1024), wg[zc, 1], preferred_element_type=F32)
        yp[zc] = acc.astype(BF)
        yd, par = zc // 2, zc % 2
        away = (y - yd + NY) % NY

        @pl.when(away == 2)
        def _():
            start(yp.at[zc], yt.at[par], s_y.at[2], r_yt.at[par], dev(z, x, (yd + 1 + 2 * par) % NY, c))

        @pl.when(away == 3 - 2 * par)
        def _():
            start(yp.at[zc], yr.at[2 + par], s_y.at[1], r_y.at[1], dev(z, x, yd, c))

    def fwd_far(par):
        wait(yt.at[0], r_yt.at[par])
        yd = (y + 3 - 2 * par) % NY
        zc = 2 * yd + par

        def one(i, carry):
            rows = pl.ds(pl.multiple_of(192 * i, 192), 192)
            yp[zc, rows] = (yp[zc, rows].astype(F32) + yt[par, rows].astype(F32)).astype(BF)
            return carry

        lax.fori_loop(0, 4, one, 0)
        start(yp.at[zc], yr.at[par], s_y.at[0], r_y.at[0], dev(z, x, yd, c))

    def fwd(k):
        need_tok()
        for j in range(2):
            need_core(j, k)
            if 0 < k < 4:
                need_core(j, 4 + k)
        if k in (0, 4):
            forward((z + k) % NZ)
        else:
            def one(i, carry):
                forward((z + (2 * i - 1) * turn * k + NZ) % NZ)
                return carry

            lax.fori_loop(0, 2, one, 0)

    def select():
        wait(ft.at[pl.ds(0, 62)], r_l.at[0])

        def pick(p):
            for s in range(3):
                ss[3 * p + s] = ft[idx[3 * p + s]]

        def send(pz, px):
            p = pz * NX + px
            pick(p)
            start(ss.at[pl.ds(3 * p, 3)], fac.at[:, ranks_at(z), lanes_at(x)],
                  s_l.at[1], r_l.at[1], dev(pz, px, y, c))

        each_dp(send)
        pick(dp)
        own = pltpu.make_async_copy(
            ss.at[pl.ds(3 * dp, 3)], fac.at[:, ranks_at(z), lanes_at(x)], s_loc.at[0])
        own.start()
        own.wait()

    def piece(m):
        return pl.ds(pl.multiple_of(48 * m, 16), 48)

    def low():
        wait(ss.at[pl.ds(0, 93)], r_l.at[1])
        for s in range(3):
            rows = slice(128 * s, 128 * s + 128)
            a = lax.dot_general(tok[rows], fac[s, 0:64], NT, preferred_element_type=F32)
            b = lax.dot_general(cot[rows], fac[s, 64:128], NT, preferred_element_type=F32)
            lp[rows] = jnp.concatenate([a, b], axis=1)

        for k in range(1, 8):
            m = lax.rem(mp + k, 8)
            start(lp.at[piece(m)], lr.at[mp], s_m.at[0], r_m.at[0], (dp, m))
        lr[mp] = lp[piece(mp)]

    def low_sum():
        wait(lr.at[pl.ds(0, 7)], r_m.at[0])
        total = lr[0]
        for m in range(1, 8):
            total = total + lr[m]
        rank_lane = lax.broadcasted_iota(jnp.int32, (16, 128), 1) % 64
        coefs = []
        for g in range(3):
            block = dp * 3 + (mp * 48 + 16 * g) // 128
            held = jnp.full((16, 128), ranks[idx[block]], jnp.int32)
            coefs.append(jnp.where(rank_lane < held, 16.0 / held.astype(F32), 0.0))
        lo[piece(mp)] = (total * jnp.concatenate(coefs, axis=0)).astype(BF)

        for k in range(1, 8):
            start(lo.at[piece(mp)], lo.at[piece(mp)], s_m.at[1], r_m.at[1], (dp, lax.rem(mp + k, 8)))

    def grads():
        wait(lo.at[pl.ds(0, 336)], r_m.at[1])
        for s in range(3):
            rows = slice(128 * s, 128 * s + 128)
            turned = lo[rows].astype(F32).T.astype(BF)
            gs[s, 0:64] = jnp.dot(turned[64:128], tok[rows], preferred_element_type=F32).astype(BF)
            gs[s, 64:128] = jnp.dot(turned[0:64], cot[rows], preferred_element_type=F32).astype(BF)

        for h in range(2):
            def send(pz, px):
                start(gs.at[:, ranks_at(pz), part_at(px, h)], gr.at[h, pl.ds(3 * dp, 3)],
                      s_l.at[2 + h], r_l.at[2 + h], dev(pz, px, y, c))

            each_dp(send)
        for h in range(2):
            own = pltpu.make_async_copy(
                gs.at[:, ranks_at(z), part_at(x, h)], gr.at[h, pl.ds(3 * dp, 3)], s_loc.at[1])
            own.start()
            own.wait()

    def bwd(j):
        need_cot()
        for k in range(8):
            need_core(j, k)

        def one(i, carry):
            t = 4 * (i // 2) + 2 * j + i % 2
            acc = jnp.zeros((768, 256), F32)
            for n in range(8):
                acc = acc + lax.dot_general(
                    cg[n].reshape(768, 256), wg[n, i // 2, lanes_at(2 * j + i % 2), :], NT,
                    preferred_element_type=F32)
            gp[t] = acc.astype(BF).reshape(4, 192, 256)
            odd = i % 2
            ahead, back = (x + 1 + 2 * odd) % NX, (x + 3 - 2 * odd) % NX
            start(gp.at[t, (x + 2) % NX], gt.at[t], s_g.at[2], r_gt.at[t], dev(z, ahead, y, c))
            start(gp.at[t, back], gg.at[1, t], s_g.at[1], r_g.at[1, t], dev(z, back, y, c))
            return carry

        lax.fori_loop(0, 4, one, 0)

    def bwd_far(j):
        def one(i, carry):
            t = 4 * (i // 2) + 2 * j + i % 2
            ahead = (x + 1 + 2 * (i % 2)) % NX
            wait(gt.at[0], r_gt.at[t])
            gp[t, ahead] = (gp[t, ahead].astype(F32) + gt[t].astype(F32)).astype(BF)
            start(gp.at[t, ahead], gg.at[0, t], s_g.at[0], r_g.at[0, t], dev(z, ahead, y, c))
            return carry

        lax.fori_loop(0, 4, one, 0)

    def sum_y():
        wait(yr.at[pl.ds(0, 2)], r_y.at[0])
        wait(yr.at[pl.ds(2, 2)], r_y.at[1])

        def one(i, carry):
            cc, px = i // 4, i % 4
            rows = pl.ds(pl.multiple_of(192 * px, 192), 192)
            acc = yp[2 * y + cc, rows].astype(F32)
            for d in range(2):
                acc = acc + yr[2 * d + cc, rows].astype(F32)
            ys[cc, px] = acc.astype(BF)
            return carry

        lax.fori_loop(0, 8, one, 0)

        def send(j, carry):
            px, pc = (x + j // 2) % NX, (c + j % 2) % 2
            start(ys.at[pc, px], yf.at[c, :, lanes_at(x)], s_ya.at[j], r_ya.at[j], dev(z, px, y, pc))
            return carry

        lax.fori_loop(1, 8, send, 0)
        own = pltpu.make_async_copy(ys.at[c, x], yf.at[c, :, lanes_at(x)], s_loc.at[2])
        own.start()
        own.wait()

    def tenant_sums(h):
        wait(gr.at[h, pl.ds(0, 93)], r_l.at[2 + h])

        def one(i, carry):
            rows = pl.ds(pl.multiple_of(256 * i, 256), 256)
            acc = jnp.dot(sel[rows, :], gr[h].reshape(1536, 128), preferred_element_type=F32)
            hs[h, pl.ds(16 * i, 16)] = acc.astype(BF).reshape(16, 16, 128)
            return carry

        lax.fori_loop(0, 4, one, 0)

        def send(pz, px):
            start(hs.at[h, pl.ds(2 * (pz * NX + px), 2)], hr.at[:, ranks_at(z), part_at(x, h)],
                  s_l.at[4 + h], r_l.at[4 + h], dev(pz, px, y, c))

        each_dp(send)
        own = pltpu.make_async_copy(
            hs.at[h, pl.ds(2 * dp, 2)], hr.at[:, ranks_at(z), part_at(x, h)], s_loc.at[3])
        own.start()
        own.wait()

    def layer_result():
        for j in range(1, 8):
            wait(ys.at[0, 0], r_ya.at[j])
        for u in range(6):
            rows = slice(64 * u, 64 * u + 64)
            acc = jnp.dot(lo[rows, 0:64], fac[u // 2, 64:128], preferred_element_type=F32)
            part = slice(64 * (u % 3), 64 * (u % 3) + 64)
            o_y[rows] = (acc + yf[u // 3, part].astype(F32)).astype(BF)
        pltpu.make_async_copy(o_y, y_out, s_io.at[5]).start()

    def sum_x(t):
        for d in range(2):
            wait(gg.at[0, 0], r_g.at[d, t])
        acc = gp[t, x].astype(F32)
        for d in range(2):
            acc = acc + gg[d, t].astype(F32)
        return acc

    def adapter_grad(h, i, q):
        rows = pl.ds(pl.multiple_of(192 * h + 64 * q, 64), 64)
        part = lo[rows, :][:, 64:128]
        return rows, jnp.dot(part, fac[(192 * h + 64 * q) // 128, 0:64, 256 * i:256 * i + 256],
                             preferred_element_type=F32)

    def grad_sums(j):
        for i in (2 * j, 2 * j + 1):
            ge[i] = sum_x(4 * o + i).astype(BF)
            start(ge.at[i], gx.at[i], s_gx.at[i], r_gx.at[i], dev(z, x, y, o))
        for i in (2 * j, 2 * j + 1):
            total = sum_x(4 * c + i)
            for q in range(3):
                rows, acc = adapter_grad(c, i, q)
                o_g[rows, 256 * i:256 * i + 256] = (acc + total[64 * q:64 * q + 64]).astype(BF)

    def grad_result(j):
        for i in (2 * j, 2 * j + 1):
            wait(ge.at[0], r_gx.at[i])
            for q in range(3):
                rows, acc = adapter_grad(o, i, q)
                part = gx[i, 64 * q:64 * q + 64].astype(F32)
                o_g[rows, 256 * i:256 * i + 256] = (acc + part).astype(BF)
        if j == 1:
            pltpu.make_async_copy(o_g, g_out, s_io.at[6]).start()

    def factor_result():
        for h in range(2):
            wait(hs.at[h, pl.ds(0, 62)], r_l.at[4 + h])
        pltpu.make_async_copy(hr, f_out, s_io.at[7]).start()

    table = {
        "spread": spread,
        "w_own": w_own,
        "ring": ring,
        "tok_out": tok_out,
        "tok_pass": tok_pass,
        "cot_out": cot_out,
        "own_copies": own_copies,
        "cot_pass": cot_pass,
        "one_hot": one_hot,
        "fwd": fwd,
        "fwd_far": fwd_far,
        "bwd_far": bwd_far,
        "cot_far": cot_far,
        "select": select,
        "low": low,
        "low_sum": low_sum,
        "grads": grads,
        "bwd": bwd,
        "sum_y": sum_y,
        "tenant_sums": tenant_sums,
        "layer_result": layer_result,
        "grad_sums": grad_sums,
        "grad_result": grad_result,
        "factor_result": factor_result,
    }
    for name, *at in ORDER:
        table[name](*at)

    for i, (a, b) in enumerate(((o_y, y_out), (o_g, g_out), (hr, f_out))):
        pltpu.make_async_copy(a, b, s_io.at[5 + i]).wait()

    wait(ft.at[pl.ds(0, 62)], s_l.at[0])
    wait(ss.at[pl.ds(0, 93)], s_l.at[1])
    for h in range(2):
        wait(gr.at[h, pl.ds(0, 93)], s_l.at[2 + h])
        wait(hs.at[h, pl.ds(0, 62)], s_l.at[4 + h])
    wait(lr.at[pl.ds(0, 7)], s_m.at[0])
    wait(lo.at[pl.ds(0, 336)], s_m.at[1])
    for j in range(2):
        rows = w.at[pl.ds(0, 512)]
        for k in range(4):
            wait(rows, s_wa.at[j, k])
        for k in range(3):
            wait(rows, s_wb.at[j, k])
        for k in range(8):
            wait(rows, s_wc.at[j, k])
    for k in range(7):
        wait(xg.at[0, 0], s_x.at[k])
    for k in range(1, 8):
        wait(cg.at[0, 0], s_c.at[k])
        wait(ys.at[0, 0], s_ya.at[k])
    for d in range(6):
        wait(cg.at[0], s_ca.at[d])
    for d in range(2):
        wait(gg.at[0], s_g.at[d])
        wait(yr.at[pl.ds(0, 2)], s_y.at[d])
    wait(gt, s_g.at[2])
    wait(yt, s_y.at[2])
    for i in range(4):
        wait(ge.at[0], s_gx.at[i])


def hand_over(y_in, g_in, f_in, y_out, g_out, dg_out, ug_out, y, g, f, dg, ug, arrived, left):
    inward = [
        pltpu.make_async_copy(a, b, arrived.at[i])
        for i, (a, b) in enumerate(((f_in, f), (y_in, y), (g_in, g)))
    ]
    outward = [
        pltpu.make_async_copy(a, b, left.at[i])
        for i, (a, b) in enumerate(((y, y_out), (g, g_out), (dg, dg_out), (ug, ug_out)))
    ]
    for copy in inward:
        copy.start()
    inward[0].wait()
    dg[...] = f[:, 0:64].astype(F32)
    outward[2].start()
    ug[...] = f[:, 64:128].astype(F32)
    outward[3].start()
    for i in range(2):
        inward[1 + i].wait()
        outward[i].start()
    for copy in outward:
        copy.wait()


def local(tokens, weight, down, up, cotangent, idx, ranks):
    down_t = jnp.swapaxes(down, 1, 2)
    up_t = jnp.swapaxes(up, 1, 2)
    anywhere = pl.BlockSpec(memory_space=pl.ANY)
    smem = pl.BlockSpec(memory_space=pltpu.SMEM)
    buf = lambda *shape: pltpu.VMEM(shape, BF)
    dma = lambda *shape: pltpu.SemaphoreType.DMA(shape)
    scratch = [
        buf(32, 2, 16, 256), buf(64, 16, 256), buf(96, 16, 256), buf(3, 128, 1024),
        buf(3, 128, 1024), buf(2, 96, 16, 128), buf(1024, 1536), buf(2, 64, 16, 128),
        buf(2, 128, 1024), pltpu.VMEM((384, 128), F32), pltpu.VMEM((8, 48, 128), F32),
        buf(384, 128),
        buf(8, 2, 1024, 256), buf(2, 4, 192, 1024), buf(8, 4, 192, 256),
        buf(8, 768, 256), buf(2, 768, 256), buf(4, 768, 256), buf(2, 4, 192, 256), buf(2, 192, 1024),
        buf(8, 4, 192, 256), buf(8, 192, 256), buf(2, 8, 192, 256), buf(4, 192, 256), buf(4, 192, 256),
        buf(384, 1024), buf(1024, 256), buf(2, 64, 1024), buf(2, 64, 1024), buf(384, 1024),
        buf(384, 1024), buf(384, 1024),
        dma(6), dma(6), dma(2, 4), dma(2, 4), dma(2, 3), dma(2, 3), dma(2, 8), dma(2, 8), dma(7), dma(7),
        dma(8), dma(8), dma(6), dma(6),
        dma(3), dma(2), dma(2), dma(8), dma(8), dma(3), dma(2, 8), dma(8), dma(4), dma(4), dma(2), dma(2),
        dma(4), dma(9),
    ]
    out = jax.ShapeDtypeStruct
    shapes = (
        out(tokens.shape, BF), out(cotangent.shape, BF), out(down_t.shape, F32), out(up_t.shape, F32),
    )
    factors = out((2, 128, 1024), BF)
    results = pl.pallas_call(
        kernel,
        out_shape=shapes[:2] + (factors,),
        in_specs=[smem, smem] + [anywhere] * 5,
        out_specs=(anywhere,) * 3,
        scratch_shapes=scratch,
        compiler_params=pltpu.CompilerParams(
            collective_id=0, has_side_effects=True, vmem_limit_bytes=60 * 1024 * 1024),
        cost_estimate=pl.CostEstimate(
            flops=13_500_000_000, bytes_accessed=6_000_000, transcendentals=0),
        name="lora_projection",
    )(idx, ranks, tokens, weight, down_t, up_t, cotangent)
    layer_out, input_grad, down_grad, up_grad = pl.pallas_call(
        hand_over,
        out_shape=shapes,
        in_specs=[anywhere] * 3,
        out_specs=(anywhere,) * 4,
        scratch_shapes=[
            pltpu.VMEM(a.shape, a.dtype) for a in shapes[:2] + (factors,) + shapes[2:]
        ] + [dma(3), dma(4)],
        name="hand_over",
    )(*results)
    return layer_out, input_grad, jnp.swapaxes(down_grad, 1, 2), jnp.swapaxes(up_grad, 1, 2)


def solution(mesh):
    return jax.shard_map(
        local,
        mesh=mesh,
        in_specs=(
            P("dp", "mp"),
            P("mp", "dp"),
            P("dp", "mp", None),
            P("dp", "mp", None),
            P("dp", "mp"),
            P(),
            P(),
        ),
        out_specs=(P("dp", "mp"), P("dp", "mp"), P("dp", "mp", None), P("dp", "mp", None)),
        check_vma=False,
    )
```
